256 devices in a mesh: row: 16 (over z, core), col: 8 (over y, x_hi), batch: 2 (over x_lo).
Axes of the slice: x: 4 (x_hi: 2, x_lo: 2; x = x_hi * 2 + x_lo), y: 4, z: 8, core: 2. Of those that a mesh axis runs over, the one named last changes fastest.
Arguments:
- fine: bfloat16 [2, 1024, 1536], P('batch', 'row'), may hold values from -6 to 6
- conv_w: bfloat16 [5, 1536, 1536], P(None, 'col'), may hold values from -0.0625 to 0.0625
- proj_a: bfloat16 [1536, 128], P('col'), may hold values from -0.15625 to 0.15625
- proj_b: bfloat16 [1536, 128], P('col'), may hold values from -0.15625 to 0.15625
- pair_in: bfloat16 [2, 512, 512, 128], P('batch', 'row', 'col'), may hold values from -6 to 6
- pair_w: bfloat16 [3, 3, 128, 128], replicated, may hold values from -0.1875 to 0.1875
- cotangent: bfloat16 [2, 512, 512, 128], P('batch', 'row', 'col'), may hold values from -1.5 to 1.5
Outputs:
- pair_out: bfloat16 [2, 512, 512, 128], P('batch', 'row', 'col')
- grad_fine: bfloat16 [2, 1024, 1536], P('batch', 'row', 'col')
- grad_pair_w: float32 [3, 3, 128, 128], replicated
The draws below stay inside these ranges and needn't reach their ends.
All inputs are finite; a program needn't handle non-finite values.
Results may differ from the reference program's by a relative error of at most 0.025.
Values may be sent and summed in bfloat16 or wider, within the bound.
No kernel may reach another device: no remote copies, remote signals or barrier semaphores. Data moves between devices by JAX's collectives and lax.ppermute only.
A program may use at most 128 MiB of HBM per device.

```python
import jax
import jax.numpy as jnp
from jax import lax

CHAN = 1536
PAIR = 128
BINS = 512
FINE = 1024
SEQS = 2


def steps_of(rng, dims, pieces, least, top_value):
    factor_of = 1.0
    for dim, blocks in pieces:
        draws = jax.random.uniform(jax.random.fold_in(jax.random.fold_in(rng, 6), dim), (blocks,), jnp.float32, least / len(pieces), top_value / len(pieces))
        factor_of = factor_of * jnp.repeat(jnp.exp(draws), dims[dim] // blocks).reshape((-1,) + (1,) * (len(dims) - 1 - dim))
    return factor_of


def gaussian(own_key, shape, width, limit, pieces=(), dtype=jnp.bfloat16):
    factor_of = steps_of(own_key, shape, pieces, -0.22, 0.18) if pieces else 1.0
    entries = jax.random.normal(own_key, shape, jnp.float32) * width * factor_of
    return jnp.minimum(jnp.maximum(entries, -limit), limit).astype(dtype)


def setup_inputs(seed: int = 0) -> dict:
    keys = jax.random.split(jax.random.key(seed), 8)
    return {
        "fine": gaussian(keys[0], (SEQS, FINE, CHAN), 1.0, 6.0, ((0, 2), (1, 16))),
        "conv_w": gaussian(keys[1], (5, CHAN, CHAN), (5 * CHAN) ** -0.5, 0.0625, ((1, 8),)),
        "proj_a": gaussian(keys[2], (CHAN, PAIR), CHAN ** -0.5, 0.15625, ((0, 8),)),
        "proj_b": gaussian(keys[3], (CHAN, PAIR), CHAN ** -0.5, 0.15625, ((0, 8),)),
        "pair_in": gaussian(keys[4], (SEQS, BINS, BINS, PAIR), 1.0, 6.0, ((0, 2), (1, 16), (2, 8))),
        "pair_w": gaussian(keys[5], (3, 3, PAIR, PAIR), (9 * PAIR) ** -0.5, 0.1875),
        "cotangent": gaussian(keys[6], (SEQS, BINS, BINS, PAIR), 0.25, 1.5, ((0, 2), (1, 16), (2, 8))),
    }


def pair_one(items, proj_w):
    pair_tile, cot_tile, row_proj, col_proj = items
    side = pair_tile.shape[0]
    chans = pair_tile.shape[2]
    zeta = (pair_tile.astype(jnp.float32) + row_proj[:, None, :] * col_proj[None, :, :]).astype(jnp.bfloat16)
    zpad = jnp.pad(zeta, ((1, 1), (1, 1), (0, 0)))
    hidden = jnp.zeros((side * side, chans), jnp.float32)
    for down in range(3):
        for across in range(3):
            piece = zpad[down:down + side, across:across + side].reshape(-1, chans)
            hidden = hidden + jnp.dot(piece, proj_w[down, across], preferred_element_type=jnp.float32)
    hidden = hidden.reshape(side, side, chans)
    output = (zeta.astype(jnp.float32) + jax.nn.silu(hidden)).astype(jnp.bfloat16)
    sigma = jax.nn.sigmoid(hidden)
    qgrad = (cot_tile.astype(jnp.float32) * sigma * (1.0 + hidden * (1.0 - sigma))).astype(jnp.bfloat16)
    qpad = jnp.pad(qgrad, ((1, 1), (1, 1), (0, 0)))
    flat_q = qgrad.reshape(-1, chans)
    zgrad = cot_tile.astype(jnp.float32).reshape(-1, chans)
    wgrads = []
    for down in range(3):
        for across in range(3):
            back = qpad[2 - down:2 - down + side, 2 - across:2 - across + side].reshape(-1, chans)
            zgrad = zgrad + lax.dot_general(back, proj_w[down, across], (((1,), (1,)), ((), ())), preferred_element_type=jnp.float32)
            piece = zpad[down:down + side, across:across + side].reshape(-1, chans)
            wgrads.append(lax.dot_general(piece, flat_q, (((0,), (0,)), ((), ())), preferred_element_type=jnp.float32))
    zgrad = zgrad.reshape(side, side, chans)
    rowg = jnp.sum(zgrad * col_proj[None, :, :], axis=1)
    colg = jnp.sum(zgrad * row_proj[:, None, :], axis=0)
    return output, jnp.stack(wgrads).reshape(3, 3, chans, chans), rowg, colg


def reference(fine, conv_w, proj_a, proj_b, pair_in, pair_w, cotangent):
    seqs = fine.shape[0]
    bins = pair_in.shape[1]
    chans = fine.shape[2]
    padded = jnp.pad(fine, ((0, 0), (2, 2), (0, 0))).reshape(seqs, bins + 2, 2, chans)
    windows = [padded[:, 0:bins, 0], padded[:, 0:bins, 1], padded[:, 1:bins + 1, 0], padded[:, 1:bins + 1, 1], padded[:, 2:bins + 2, 0]]
    seq_acc = jnp.zeros((seqs * bins, chans), jnp.float32)
    for index in range(5):
        seq_acc = seq_acc + lax.dot_general(windows[index].reshape(-1, chans), conv_w[index], (((1,), (1,)), ((), ())), preferred_element_type=jnp.float32)
    seq = seq_acc.astype(jnp.bfloat16)
    rowp = jnp.dot(seq, proj_a, preferred_element_type=jnp.float32).reshape(seqs, bins, -1)
    colp = jnp.dot(seq, proj_b, preferred_element_type=jnp.float32).reshape(seqs, bins, -1)
    outputs, wgrads, rowg, colg = lax.map(lambda items: pair_one(items, pair_w), (pair_in, cotangent, rowp, colp))
    grad_pair_w = jnp.sum(wgrads, axis=0) / bins
    pairs = rowg.shape[2]
    seqg = (jnp.dot(rowg.reshape(-1, pairs), proj_a.T.astype(jnp.float32), preferred_element_type=jnp.float32)
            + jnp.dot(colg.reshape(-1, pairs), proj_b.T.astype(jnp.float32), preferred_element_type=jnp.float32)).astype(jnp.bfloat16)
    seqg = jnp.pad(seqg.reshape(seqs, bins, chans), ((0, 0), (1, 1), (0, 0))).reshape(-1, chans)
    taps = [jnp.dot(seqg, conv_w[index], preferred_element_type=jnp.float32).reshape(seqs, bins + 2, chans) for index in range(5)]
    even = taps[0][:, 2:bins + 2] + taps[2][:, 1:bins + 1] + taps[4][:, 0:bins]
    odd = taps[1][:, 2:bins + 2] + taps[3][:, 1:bins + 1]
    grad_fine = jnp.stack((even, odd), axis=2).reshape(seqs, 2 * bins, chans).astype(jnp.bfloat16)
    return outputs, grad_fine, grad_pair_w
```

```python
import jax
import jax.numpy as jnp
from jax import lax
from jax.sharding import PartitionSpec as P

BF = jnp.bfloat16
F32 = jnp.float32
WIDE = 80


def shift(x, axis, step):
    count = lax.axis_size(axis)
    return lax.ppermute(x, axis, [(i, (i + step) % count) for i in range(count)])


def flip(x, axis, bit):
    count = lax.axis_size(axis)
    return lax.ppermute(x, axis, [(i, i ^ bit) for i in range(count)])


def ring(x, step):
    pairs = [(4 * y + p, 4 * y + (p + step) % 4) for y in range(4) for p in range(4)]
    return lax.ppermute(x, ("col", "batch"), pairs)


def up(x):
    return x.astype(F32)


def sum_y(x):
    across, left, right = shift(x, "col", 4), shift(x, "col", 2), shift(x, "col", 6)
    return ((up(x) + up(across)) + (up(left) + up(right))).astype(BF)


def sum_x(x):
    across, left, right = flip(x, "col", 1), ring(x, 1), ring(x, 3)
    return ((up(x) + up(across)) + (up(left) + up(right))).astype(BF)


def sum_flip(x, axis, bit):
    return (up(x) + up(flip(x, axis, bit))).astype(BF)


def turned(x, step):
    return jnp.roll(x, -step, axis=1)


def pair_block(pair_ext, cot_ext, rowp, colp, row_ok, col_ok, pair_w):
    chans = pair_ext.shape[-1]
    ok = row_ok[:, None, None] & col_ok[None, :, None]
    zeta = jnp.where(ok, up(pair_ext) + rowp[:, None, :] * colp[None, :, :], 0.0).astype(BF)
    cot = jnp.where(ok[1:37], up(cot_ext), 0.0)
    z3 = jnp.concatenate([turned(zeta, -1), zeta, turned(zeta, 1)], axis=-1)
    hidden = 0.0
    for down in range(3):
        hidden = hidden + jnp.dot(
            z3[down : down + 36].reshape(-1, 3 * chans),
            pair_w[down].reshape(3 * chans, chans),
            preferred_element_type=F32,
        )
    hidden = hidden.reshape(36, WIDE, chans)
    sigma = jax.nn.sigmoid(hidden)
    own_h = hidden[2:34, :64]
    out = (up(zeta[3:35, :64]) + own_h * sigma[2:34, :64]).astype(BF)
    q = (cot * sigma * (1.0 + hidden * (1.0 - sigma))).astype(BF)
    q3 = jnp.concatenate([turned(q, 1), q, turned(q, -1)], axis=-1)
    zgrad = cot[1:35].reshape(-1, chans)
    flat_q = q[2:34, :64].reshape(-1, chans)
    wgrads = []
    for down in range(3):
        zgrad = zgrad + jnp.dot(
            q3[2 - down : 36 - down].reshape(-1, 3 * chans),
            jnp.swapaxes(pair_w[down], 1, 2).reshape(3 * chans, chans),
            preferred_element_type=F32,
        )
        wgrads.append(
            lax.dot_general(
                z3[down + 2 : down + 34, :64].reshape(-1, 3 * chans),
                flat_q,
                (((0,), (0,)), ((), ())),
                preferred_element_type=F32,
            )
        )
    zgrad = zgrad.reshape(34, WIDE, chans)
    row_part = jnp.sum(zgrad[:, :64] * colp[None, :64, :], axis=1)
    row_part = jnp.where(row_ok[2:36, None], row_part, 0.0)
    col_part = jnp.sum(zgrad[1:33] * rowp[3:35, None, :], axis=0)
    col_part = jnp.where(col_ok[:, None], col_part, 0.0)
    return out, jnp.concatenate(wgrads), row_part, col_part


def local(fine, conv_w, proj_a, proj_b, pair_in, pair_w, cotangent):
    chans, outchans, pairs = fine.shape[2], conv_w.shape[1], pair_in.shape[3]
    row, col = lax.axis_index("row"), lax.axis_index("col")
    core, zpos = row % 2, row // 2
    first, last = row == 0, row == 15
    row_bins = 32 * row - 3 + jnp.arange(38)
    row_ok = (row_bins >= 0) & (row_bins < 512)
    place = jnp.arange(WIDE)
    bins = 64 * col + jnp.where(place < 72, place, place - WIDE)
    col_ok = (bins >= 0) & (bins < 512)

    fine = fine[0]
    before = jnp.where(first, 0, shift(fine[-8:], "row", 1))
    after = jnp.where(last, 0, shift(fine[:8], "row", -1))
    grouped = jnp.concatenate([before, fine, after]).reshape(40, 2, chans)
    seq = 0.0
    for tap in range(5):
        seq = seq + lax.dot_general(
            grouped[tap // 2 : tap // 2 + 38, tap % 2],
            conv_w[tap],
            (((1,), (1,)), ((), ())),
            preferred_element_type=F32,
        )
    seq = jnp.where(row_ok[:, None], seq, 0.0).astype(BF)
    proj = jnp.concatenate([proj_a, proj_b], axis=1)
    part = jnp.dot(seq, proj, preferred_element_type=F32).astype(BF)
    both = up(sum_flip(sum_y(part), "col", 1))
    rowp, colp_here = both[:, :pairs], both[:, pairs:].astype(BF)

    mine = jnp.where(core == 0, colp_here[:35], colp_here[3:])
    other = flip(mine, "row", 1)
    colp = jnp.concatenate(
        [jnp.where(core == 0, mine, other), jnp.where(core == 0, other, mine)]
    )
    apart = zpos ^ col
    for bit in (4, 2, 1):
        colp = jnp.where((apart & (2 * bit - 1)) == bit, flip(colp, "row", 2 * bit), colp)
    colp = up(jnp.concatenate([colp[3:], jnp.zeros((10, pairs), BF), colp[:3]]))

    pair, cot = pair_in[0], cotangent[0]
    left = shift(jnp.concatenate([pair[:, 61:], cot[:, 62:]], axis=1), "col", 1)
    right = shift(jnp.concatenate([pair[:, :3], cot[:, :2]], axis=1), "col", -1)
    pair_ext = jnp.concatenate(
        [pair, right[:, :3], jnp.zeros((32, 10, pairs), BF), left[:, :3]], axis=1
    )
    cot_ext = jnp.concatenate(
        [cot, right[:, 3:], jnp.zeros((32, 12, pairs), BF), left[:, 3:]], axis=1
    )
    top = shift(jnp.concatenate([pair_ext[29:], cot_ext[30:]]), "row", 1)
    bottom = shift(jnp.concatenate([pair_ext[:3], cot_ext[:2]]), "row", -1)
    pair_ext = jnp.concatenate([top[:3], pair_ext, bottom[:3]])
    cot_ext = jnp.concatenate([top[3:], cot_ext, bottom[3:]])

    out, wgrad, row_part, col_part = pair_block(
        pair_ext, cot_ext, rowp, colp, row_ok, col_ok, pair_w
    )

    half = wgrad.shape[0] // 2
    keep = jnp.where(core == 0, wgrad[:half], wgrad[half:])
    send = jnp.where(core == 0, wgrad[half:], wgrad[:half]).astype(BF)
    total = (keep + up(flip(send, "row", 1))).astype(BF)
    total = sum_x(sum_y(total))
    for bit in (2, 4, 8):
        total = sum_flip(total, "row", bit)
    theirs = flip(total, "row", 1)
    total = jnp.concatenate([jnp.where(core == 0, total, theirs), jnp.where(core == 0, theirs, total)])
    grad_pair_w = up(total).reshape(3, 3, pairs, pairs) / 512.0

    line = jnp.concatenate([col_part[-1:], col_part[:65]])
    keep = jnp.where(core == 0, line[:34], line[32:])
    send = jnp.where(core == 0, line[32:], line[:34]).astype(BF)
    colg = (keep + up(flip(send, "row", 1))).astype(BF)
    for bit in (2, 4, 8):
        colg = sum_flip(colg, "row", bit)
    colg = jnp.where(zpos == col, colg, 0)
    sums = jnp.concatenate([row_part.astype(BF), colg], axis=1)
    sums = sum_flip(sum_y(sums), "col", 1)
    seqg = lax.dot_general(sums, proj, (((1,), (1,)), ((), ())), preferred_element_type=F32).astype(BF)
    taps = [jnp.dot(seqg, conv_w[tap], preferred_element_type=F32) for tap in range(5)]
    even = taps[0][2:] + taps[2][1:33] + taps[4][:32]
    odd = taps[1][2:] + taps[3][1:33]
    parts = jnp.stack((even, odd), axis=1).astype(BF).reshape(64, 8, outchans)
    parts = lax.all_to_all(parts.transpose(1, 0, 2), "col", 0, 0, tiled=True)
    grad_fine = jnp.sum(up(parts), axis=0).astype(BF)
    return out[None], grad_fine[None], grad_pair_w


def solution(mesh):
    return jax.shard_map(
        local,
        mesh=mesh,
        in_specs=(
            P("batch", "row", None),
            P(None, "col", None),
            P("col", None),
            P("col", None),
            P("batch", "row", "col", None),
            P(),
            P("batch", "row", "col", None),
        ),
        out_specs=(P("batch", "row", "col", None), P("batch", "row", "col"), P()),
        check_vma=False,
    )
```

```python
import jax
import jax.numpy as jnp
from jax import lax
from jax.experimental import pallas as pl
from jax.experimental.pallas import tpu as pltpu
from jax.sharding import PartitionSpec as P

BF = jnp.bfloat16
F32 = jnp.float32
WIDE = 80
KEPT = 616


def shift(x, axis, step):
    count = lax.axis_size(axis)
    return lax.ppermute(x, axis, [(i, (i + step) % count) for i in range(count)])


def flip(x, axis, bit):
    count = lax.axis_size(axis)
    return lax.ppermute(x, axis, [(i, i ^ bit) for i in range(count)])


def ring(x, step):
    pairs = [(4 * y + p, 4 * y + (p + step) % 4) for y in range(4) for p in range(4)]
    return lax.ppermute(x, ("col", "batch"), pairs)


def up(x):
    return x.astype(F32)


def sum_y(x):
    across, left, right = shift(x, "col", 4), shift(x, "col", 2), shift(x, "col", 6)
    return ((up(x) + up(across)) + (up(left) + up(right))).astype(BF)


def sum_flip(x, axis, bit):
    return (up(x) + up(flip(x, axis, bit))).astype(BF)


def pair_kernel(
    flags, pair, cot, top, bottom, left, right, rowp, colp, weight, turned,
    out, keep, send, rowg,
    zwide, z3, cots, qwide, q3, wgrad, line,
):
    chans = 128
    has_up, has_down, has_left, has_right, core = (flags[i] for i in range(5))
    rows = lax.broadcasted_iota(jnp.int32, (38, 1, 1), 0)
    row_ok = ((rows >= 3) | (has_up > 0)) & ((rows < 35) | (has_down > 0))

    zwide[:, 0:8] = jnp.zeros((38, 8, chans), F32)
    zwide[:, 72:96] = jnp.zeros((38, 24, chans), F32)
    cots[:, 64:80] = jnp.zeros((36, 16, chans), F32)

    def zeta(values, first, count, lo, hi):
        scaled = rowp[first : first + count][:, None, :] * colp[lo:hi][None, :, :]
        return up((up(values) + scaled).astype(BF))

    zwide[0:3, 8:72] = jnp.where(has_up > 0, zeta(top[0:3], 0, 3, 8, 72), 0.0)
    zwide[35:38, 8:72] = jnp.where(has_down > 0, zeta(bottom[0:3], 35, 3, 8, 72), 0.0)
    cots[0:2, 0:64] = jnp.where(has_up > 0, up(top[3:5]), 0.0)
    cots[34:36, 0:64] = jnp.where(has_down > 0, up(bottom[3:5]), 0.0)
    edge = jnp.where(row_ok & (has_left > 0), zeta(left[:, 0:3], 0, 38, 5, 8), 0.0)
    zwide[:, 5:8] = edge
    zwide[:, 85:88] = edge
    edge = jnp.where(row_ok & (has_right > 0), zeta(right[:, 0:3], 0, 38, 72, 75), 0.0)
    zwide[:, 72:75] = edge
    cots[:, 78:80] = jnp.where(row_ok[1:37] & (has_left > 0), up(left[1:37, 3:5]), 0.0)
    cots[:, 64:66] = jnp.where(row_ok[1:37] & (has_right > 0), up(right[1:37, 3:5]), 0.0)
    for at in range(0, 32, 4):
        zwide[at + 3 : at + 7, 8:72] = zeta(pair[at : at + 4], at + 3, 4, 8, 72)
        cots[at + 2 : at + 6, 0:64] = up(cot[at : at + 4])
    zwide[:, 88:89] = zwide[:, 8:9]
    for at in range(0, 38, 2):
        for across in range(3):
            z3[at : at + 2, :, across * chans : (across + 1) * chans] = zwide[
                at : at + 2, 7 + across : 87 + across
            ].astype(BF)

    qwide[:, 0:8] = jnp.zeros((36, 8, chans), F32)
    qwide[:, 88:96] = jnp.zeros((36, 8, chans), F32)
    for at in range(0, 36, 6):
        taps = jnp.concatenate([z3[at + d : at + d + 6].reshape(6 * WIDE, 3 * chans) for d in range(3)], axis=1)
        hidden = jnp.dot(taps, weight[...], preferred_element_type=F32).reshape(6, WIDE, chans)
        sigma = jax.nn.sigmoid(hidden)
        grown = hidden * sigma
        q = cots[at : at + 6] * (sigma + grown * (1.0 - sigma))
        qwide[at : at + 6, 8:88] = up(q.astype(BF))
        lo, hi = max(at, 2), min(at + 6, 34)
        out[lo - 2 : hi - 2] = (
            zwide[lo + 1 : hi + 1, 8:72] + grown[lo - at : hi - at, 0:64]
        ).astype(BF)
    qwide[:, 7:8] = qwide[:, 87:88]
    qwide[:, 88:89] = qwide[:, 8:9]
    for at in range(0, 36, 2):
        for across in range(3):
            q3[at : at + 2, :, across * chans : (across + 1) * chans] = qwide[
                at : at + 2, 9 - across : 89 - across
            ].astype(BF)

    own = q3[2:34, 0:64, chans : 2 * chans].reshape(2048, chans)
    for down in range(3):
        near = z3[down + 2 : down + 34, 0:64].reshape(2048, 3 * chans)
        part = lax.dot_general(own, near, (((0,), (0,)), ((), ())), preferred_element_type=F32)
        for across in range(3):
            at = (3 * down + across) * chans
            wgrad[at : at + chans] = part[:, across * chans : (across + 1) * chans].T

    total = jnp.zeros((WIDE, chans), F32)
    rowg[...] = jnp.zeros((40, chans), BF)
    for at in range(0, 34, 6):
        count = min(6, 34 - at)
        taps = jnp.concatenate(
            [q3[at + 2 - d : at + 2 - d + count].reshape(count * WIDE, 3 * chans) for d in range(3)], axis=1
        )
        zgrad = jnp.dot(taps, turned[...], preferred_element_type=F32).reshape(count, WIDE, chans)
        zgrad = zgrad + cots[at + 1 : at + 1 + count]
        rowg[at : at + count] = jnp.sum(zgrad[:, 0:64] * colp[8:72][None], axis=1).astype(BF)
        for i in range(count):
            if 1 <= at + i < 33:
                total = total + zgrad[i] * rowp[at + i + 2 : at + i + 3]
    rowg[0:1] = jnp.where(has_up > 0, rowg[0:1], 0.0)
    rowg[33:34] = jnp.where(has_down > 0, rowg[33:34], 0.0)
    line[0:1] = jnp.where(has_left > 0, total[79:80], 0.0)
    line[1:65] = total[0:64]
    line[65:66] = jnp.where(has_right > 0, total[64:65], 0.0)
    keep[576:616] = jnp.zeros((40, chans), F32)
    send[576:616] = jnp.zeros((40, chans), BF)
    for mine in range(2):

        @pl.when(core == mine)
        def _(mine=mine):
            keep[0:576] = wgrad[576 * mine : 576 * mine + 576]
            send[0:576] = wgrad[576 - 576 * mine : 1152 - 576 * mine].astype(BF)
            keep[576:610] = line[32 * mine : 32 * mine + 34]
            send[576:610] = line[32 - 32 * mine : 66 - 32 * mine].astype(BF)


def pair_block(flags, pair, cot, top, bottom, left, right, rowp, colp, weight, turned):
    chans = 128
    vmem = pl.BlockSpec(memory_space=pltpu.VMEM)
    return pl.pallas_call(
        pair_kernel,
        out_shape=(
            jax.ShapeDtypeStruct((32, 64, chans), BF),
            jax.ShapeDtypeStruct((KEPT, chans), F32),
            jax.ShapeDtypeStruct((KEPT, chans), BF),
            jax.ShapeDtypeStruct((40, chans), BF),
        ),
        in_specs=[pl.BlockSpec(memory_space=pltpu.SMEM)] + [vmem] * 10,
        out_specs=(vmem,) * 4,
        scratch_shapes=[
            pltpu.VMEM((38, 96, chans), F32),
            pltpu.VMEM((38, WIDE, 3 * chans), BF),
            pltpu.VMEM((36, WIDE, chans), F32),
            pltpu.VMEM((36, 96, chans), F32),
            pltpu.VMEM((36, WIDE, 3 * chans), BF),
            pltpu.VMEM((9 * chans, chans), F32),
            pltpu.VMEM((72, chans), F32),
        ],
        compiler_params=pltpu.CompilerParams(vmem_limit_bytes=40 * 1024 * 1024),
        cost_estimate=pl.CostEstimate(flops=2500000000, bytes_accessed=4000000, transcendentals=700000),
    )(flags, pair, cot, top, bottom, left, right, rowp, colp, weight, turned)


def local(fine, conv_w, proj_a, proj_b, pair_in, pair_w, cotangent):
    chans, outchans, pairs = fine.shape[2], conv_w.shape[1], pair_in.shape[3]
    row, col = lax.axis_index("row"), lax.axis_index("col")
    core, zpos = row % 2, row // 2
    first, last = row == 0, row == 15
    row_bins = 32 * row - 3 + jnp.arange(38)
    row_ok = (row_bins >= 0) & (row_bins < 512)
    flags = jnp.stack([row > 0, row < 15, col > 0, col < 7, core > 0]).astype(jnp.int32)

    fine, pair, cot = fine[0], pair_in[0], cotangent[0]
    before = shift(fine[-8:], "row", 1)
    after = shift(fine[:8], "row", -1)
    top = shift(jnp.concatenate([pair[29:], cot[30:]]), "row", 1)
    bottom = shift(jnp.concatenate([pair[:3], cot[:2]]), "row", -1)
    grouped = jnp.concatenate(
        [jnp.where(first, 0, before), fine, jnp.where(last, 0, after)]
    ).reshape(40, 2, chans)
    seq = 0.0
    for tap in range(5):
        seq = seq + lax.dot_general(
            grouped[tap // 2 : tap // 2 + 38, tap % 2],
            conv_w[tap],
            (((1,), (1,)), ((), ())),
            preferred_element_type=F32,
        )
    seq = jnp.where(row_ok[:, None], seq, 0.0).astype(BF)
    proj = jnp.concatenate([proj_a, proj_b], axis=1)
    part = jnp.dot(seq, proj, preferred_element_type=F32).astype(BF)
    part = jnp.concatenate([part, jnp.zeros((2, 2 * pairs), BF)])

    tall_pair = jnp.concatenate([top[:3], pair, bottom[:3]])
    tall_cot = jnp.concatenate([top[2:], cot, bottom[3:], bottom[4:]])
    left = shift(jnp.concatenate([tall_pair[:, 61:], tall_cot[:, 62:], tall_cot[:, :3]], axis=1), "col", 1)
    right = shift(jnp.concatenate([tall_pair[:, :3], tall_cot[:, :5]], axis=1), "col", -1)

    both = up(sum_flip(sum_y(part), "col", 1))
    rowp, colp_here = both[:, :pairs], both[:, pairs:].astype(BF)

    mine = jnp.where(core == 0, colp_here[:35], colp_here[3:38])
    other = flip(mine, "row", 1)
    colp = jnp.concatenate([jnp.where(core == 0, mine, other), jnp.where(core == 0, other, mine)])
    apart = zpos ^ col
    colp = jnp.where((apart & 4) == 4, flip(colp, "row", 8), colp)
    near = [flip(colp, "row", 2 * k) for k in (1, 2, 3)]
    for k in (1, 2, 3):
        colp = jnp.where((apart & 3) == k, near[k - 1], colp)
    blank = jnp.zeros((10, pairs), BF)
    colp = up(jnp.concatenate([blank[:5], colp[:3], colp[3:], blank, colp[:3], colp[3:4], blank[:7]]))

    weight = pair_w.reshape(9 * pairs, pairs)
    turned = jnp.swapaxes(pair_w, 2, 3).reshape(9 * pairs, pairs)
    out, keep, send, rowg = pair_block(
        flags, pair, cot, top, bottom, left, right, rowp, colp, weight, turned
    )

    total = (keep + up(flip(send, "row", 1))).astype(BF)
    half, colg = total[:576].reshape(4, 144, pairs), total[576:]

    def quarter(k):
        return lax.dynamic_index_in_dim(half, (zpos ^ k) & 3, 0, keepdims=False)

    def joined(k):
        return jnp.concatenate([quarter(k), colg])

    got = [flip(joined(k), "row", 2 * k) for k in (1, 2, 3)]
    total = ((up(joined(0)) + up(got[0])) + (up(got[1]) + up(got[2]))).astype(BF)
    total = sum_flip(total, "row", 8)
    colg = jnp.where(zpos == col, total[144:], 0)
    total = sum_y(jnp.concatenate([total[:144], rowg, colg]))
    across, left, right = flip(total, "col", 1), ring(total[:144], 1), ring(total[:144], 3)
    total = up(total) + up(across)
    sums = total[144:].astype(BF)
    quart = (total[:144] + (up(left) + up(right))).astype(BF)

    near = jnp.stack([quart] + [flip(quart, "row", 2 * k) for k in (1, 2, 3)])
    half = jnp.concatenate([lax.dynamic_index_in_dim(near, (zpos ^ k) & 3, 0, keepdims=False) for k in range(4)])
    theirs = flip(half, "row", 1)
    grad_pair_w = jnp.concatenate([jnp.where(core == 0, half, theirs), jnp.where(core == 0, theirs, half)])
    grad_pair_w = up(grad_pair_w).reshape(3, 3, pairs, pairs) / 512.0

    sums = jnp.concatenate([sums[:34], sums[40:74]], axis=1)
    seqg = lax.dot_general(sums, proj, (((1,), (1,)), ((), ())), preferred_element_type=F32).astype(BF)
    taps = [jnp.dot(seqg, conv_w[tap], preferred_element_type=F32) for tap in range(5)]
    even = taps[0][2:] + taps[2][1:33] + taps[4][:32]
    odd = taps[1][2:] + taps[3][1:33]
    parts = jnp.stack((even, odd), axis=1).astype(BF).reshape(64, 8, outchans)
    parts = lax.all_to_all(parts.transpose(1, 0, 2), "col", 0, 0, tiled=True)
    grad_fine = jnp.sum(up(parts), axis=0).astype(BF)
    return out[None], grad_fine[None], grad_pair_w


def solution(mesh):
    return jax.shard_map(
        local,
        mesh=mesh,
        in_specs=(
            P("batch", "row", None),
            P(None, "col", None),
            P("col", None),
            P("col", None),
            P("batch", "row", "col", None),
            P(),
            P("batch", "row", "col", None),
        ),
        out_specs=(P("batch", "row", "col", None), P("batch", "row", "col"), P()),
        check_vma=False,
    )
```

```python
import jax
import jax.numpy as jnp
from jax import lax
from jax.experimental import pallas as pl
from jax.experimental.pallas import tpu as pltpu
from jax.sharding import PartitionSpec as P

BF = jnp.bfloat16
F32 = jnp.float32
WIDE = 80
KEPT = 616


def shift(x, axis, step):
    count = lax.axis_size(axis)
    return lax.ppermute(x, axis, [(i, (i + step) % count) for i in range(count)])


def flip(x, axis, bit):
    count = lax.axis_size(axis)
    return lax.ppermute(x, axis, [(i, i ^ bit) for i in range(count)])


def up(x):
    return x.astype(F32)


def sum_y(x):
    across, left, right = shift(x, "col", 4), shift(x, "col", 2), shift(x, "col", 6)
    return ((up(x) + up(across)) + (up(left) + up(right))).astype(BF)


def sum_flip(x, axis, bit):
    return (up(x) + up(flip(x, axis, bit))).astype(BF)


def taken(x, at):
    return lax.dynamic_slice(x, (at, 0, 0), (1,) + x.shape[1:], allow_negative_indices=False)[0]


def pair_kernel(
    flags, pair, cot, top, bottom, left, right, rowp, bins, weight,
    out, keep, send, rowg,
    zwide, z3, cots, qwide, q3, wgrad, line, colp, turned,
):
    chans = 128
    has_up, has_down, has_left, has_right, core = (flags[i] for i in range(5))
    rows = lax.broadcasted_iota(jnp.int32, (38, 1, 1), 0)
    row_ok = ((rows >= 3) | (has_up > 0)) & ((rows < 35) | (has_down > 0))

    colp[...] = jnp.zeros((96, chans), F32)
    colp[5:75] = bins[0:70]
    colp[85:88] = bins[0:3]
    colp[88:89] = bins[3:4]
    for at in range(0, 9 * chans, chans):
        turned[at : at + chans] = up(weight[at : at + chans]).T.astype(BF)

    zwide[:, 0:8] = jnp.zeros((38, 8, chans), F32)
    zwide[:, 72:96] = jnp.zeros((38, 24, chans), F32)
    cots[:, 64:80] = jnp.zeros((36, 16, chans), F32)

    def zeta(values, first, count, lo, hi):
        scaled = rowp[first : first + count][:, None, :] * colp[lo:hi][None, :, :]
        return up((up(values) + scaled).astype(BF))

    zwide[0:3, 8:72] = jnp.where(has_up > 0, zeta(top[0:3], 0, 3, 8, 72), 0.0)
    zwide[35:38, 8:72] = jnp.where(has_down > 0, zeta(bottom[0:3], 35, 3, 8, 72), 0.0)
    cots[0:2, 0:64] = jnp.where(has_up > 0, up(top[3:5]), 0.0)
    cots[34:36, 0:64] = jnp.where(has_down > 0, up(bottom[3:5]), 0.0)
    edge = jnp.where(row_ok & (has_left > 0), zeta(left[:, 0:3], 0, 38, 5, 8), 0.0)
    zwide[:, 5:8] = edge
    zwide[:, 85:88] = edge
    edge = jnp.where(row_ok & (has_right > 0), zeta(right[:, 0:3], 0, 38, 72, 75), 0.0)
    zwide[:, 72:75] = edge
    cots[:, 78:80] = jnp.where(row_ok[1:37] & (has_left > 0), up(left[1:37, 3:5]), 0.0)
    cots[:, 64:66] = jnp.where(row_ok[1:37] & (has_right > 0), up(right[1:37, 3:5]), 0.0)
    for at in range(0, 32, 4):
        zwide[at + 3 : at + 7, 8:72] = zeta(pair[at : at + 4], at + 3, 4, 8, 72)
        cots[at + 2 : at + 6, 0:64] = up(cot[at : at + 4])
    zwide[:, 88:89] = zwide[:, 8:9]
    for at in range(0, 38, 2):
        for across in range(3):
            z3[at : at + 2, :, across * chans : (across + 1) * chans] = zwide[
                at : at + 2, 7 + across : 87 + across
            ].astype(BF)

    qwide[:, 0:8] = jnp.zeros((36, 8, chans), F32)
    qwide[:, 88:96] = jnp.zeros((36, 8, chans), F32)
    for at in range(0, 36, 6):
        taps = jnp.concatenate([z3[at + d : at + d + 6].reshape(6 * WIDE, 3 * chans) for d in range(3)], axis=1)
        hidden = jnp.dot(taps, weight[...], preferred_element_type=F32).reshape(6, WIDE, chans)
        sigma = jax.nn.sigmoid(hidden)
        grown = hidden * sigma
        q = cots[at : at + 6] * (sigma + grown * (1.0 - sigma))
        qwide[at : at + 6, 8:88] = up(q.astype(BF))
        lo, hi = max(at, 2), min(at + 6, 34)
        out[lo - 2 : hi - 2] = (
            zwide[lo + 1 : hi + 1, 8:72] + grown[lo - at : hi - at, 0:64]
        ).astype(BF)
    qwide[:, 7:8] = qwide[:, 87:88]
    qwide[:, 88:89] = qwide[:, 8:9]
    for at in range(0, 36, 2):
        for across in range(3):
            q3[at : at + 2, :, across * chans : (across + 1) * chans] = qwide[
                at : at + 2, 9 - across : 89 - across
            ].astype(BF)

    own = q3[2:34, 0:64, chans : 2 * chans].reshape(2048, chans)
    for down in range(3):
        near = z3[down + 2 : down + 34, 0:64].reshape(2048, 3 * chans)
        part = lax.dot_general(own, near, (((0,), (0,)), ((), ())), preferred_element_type=F32)
        for across in range(3):
            at = (3 * down + across) * chans
            wgrad[at : at + chans] = part[:, across * chans : (across + 1) * chans].T

    total = jnp.zeros((WIDE, chans), F32)
    rowg[...] = jnp.zeros((40, chans), BF)
    for at in range(0, 34, 6):
        count = min(6, 34 - at)
        taps = jnp.concatenate(
            [q3[at + 2 - d : at + 2 - d + count].reshape(count * WIDE, 3 * chans) for d in range(3)], axis=1
        )
        zgrad = jnp.dot(taps, turned[...], preferred_element_type=F32).reshape(count, WIDE, chans)
        zgrad = zgrad + cots[at + 1 : at + 1 + count]
        rowg[at : at + count] = jnp.sum(zgrad[:, 0:64] * colp[8:72][None], axis=1).astype(BF)
        for i in range(count):
            if 1 <= at + i < 33:
                total = total + zgrad[i] * rowp[at + i + 2 : at + i + 3]
    rowg[0:1] = jnp.where(has_up > 0, rowg[0:1], 0.0)
    rowg[33:34] = jnp.where(has_down > 0, rowg[33:34], 0.0)
    line[0:1] = jnp.where(has_left > 0, total[79:80], 0.0)
    line[1:65] = total[0:64]
    line[65:66] = jnp.where(has_right > 0, total[64:65], 0.0)
    keep[576:616] = jnp.zeros((40, chans), F32)
    send[576:616] = jnp.zeros((40, chans), BF)
    for mine in range(2):

        @pl.when(core == mine)
        def _(mine=mine):
            keep[0:576] = wgrad[576 * mine : 576 * mine + 576]
            send[0:576] = wgrad[576 - 576 * mine : 1152 - 576 * mine].astype(BF)
            keep[576:610] = line[32 * mine : 32 * mine + 34]
            send[576:610] = line[32 - 32 * mine : 66 - 32 * mine].astype(BF)


def conv_kernel(flags, fine, before, after, conv_w, proj, part, wide):
    blocks = wide.shape[0]
    wide[:, 80:88] = jnp.zeros((blocks, 8, 128), F32)
    for j in range(blocks):
        lanes = slice(128 * j, 128 * j + 128)
        wide[j, 0:8] = jnp.where(flags[0] > 0, up(before[:, lanes]), 0.0)
        wide[j, 8:72] = up(fine[:, lanes])
        wide[j, 72:80] = jnp.where(flags[1] > 0, up(after[:, lanes]), 0.0)
    seq = jnp.zeros((40, conv_w.shape[1]), F32)
    for tap in range(5):
        window = jnp.concatenate([wide[j, pl.ds(tap, 40, stride=2)] for j in range(blocks)], axis=1)
        seq = seq + lax.dot_general(
            window.astype(BF), conv_w[tap], (((1,), (1,)), ((), ())), preferred_element_type=F32
        )
    rows = lax.broadcasted_iota(jnp.int32, (40, 1), 0)
    ok = ((rows >= 3) | (flags[0] > 0)) & ((rows < 35) | (flags[1] > 0)) & (rows < 38)
    seq = jnp.where(ok, seq, 0.0).astype(BF)
    part[...] = jnp.dot(seq, proj[...], preferred_element_type=F32).astype(BF)


def grad_conv_kernel(sums, proj, conv_w, parts, seqg, whole):
    pair = jnp.concatenate([sums[0:40], sums[40:80]], axis=1)
    grad = lax.dot_general(pair, proj[...], (((1,), (1,)), ((), ())), preferred_element_type=F32)
    seqg[...] = up(grad.astype(BF))
    ahead, here, behind = (seqg[at : at + 32].astype(BF) for at in (2, 1, 0))

    def times(x, tap):
        return jnp.dot(x, conv_w[tap], preferred_element_type=F32)

    even = times(ahead, 0) + times(here, 2) + times(behind, 4)
    odd = times(ahead, 1) + times(here, 3)
    for j in range(whole.shape[0]):
        lanes = slice(128 * j, 128 * j + 128)
        whole[j, pl.ds(0, 32, stride=2)] = even[:, lanes]
        whole[j, pl.ds(1, 32, stride=2)] = odd[:, lanes]
    for m in range(4):
        low, middle, high = (whole[3 * m + i] for i in range(3))
        parts[2 * m] = jnp.concatenate([low, middle[:, :64]], axis=1).astype(BF)
        parts[2 * m + 1] = jnp.concatenate([middle[:, 64:], high], axis=1).astype(BF)


VMEM = pl.BlockSpec(memory_space=pltpu.VMEM)
SMEM = pl.BlockSpec(memory_space=pltpu.SMEM)


def conv_forward(flags, fine, before, after, conv_w, proj):
    chans = fine.shape[1]
    return pl.pallas_call(
        conv_kernel,
        out_shape=jax.ShapeDtypeStruct((40, proj.shape[1]), BF),
        in_specs=[SMEM] + [VMEM] * 5,
        out_specs=VMEM,
        scratch_shapes=[pltpu.VMEM((chans // 128, 88, 128), F32)],
        compiler_params=pltpu.CompilerParams(vmem_limit_bytes=12 * 1024 * 1024),
        cost_estimate=pl.CostEstimate(flops=120000000, bytes_accessed=3500000, transcendentals=0),
    )(flags, fine, before, after, conv_w, proj)


def conv_backward(sums, proj, conv_w):
    outchans, chans = conv_w.shape[1:]
    return pl.pallas_call(
        grad_conv_kernel,
        out_shape=jax.ShapeDtypeStruct((8, 64, outchans), BF),
        in_specs=[VMEM] * 3,
        out_specs=VMEM,
        scratch_shapes=[pltpu.VMEM((40, outchans), F32), pltpu.VMEM((chans // 128, 64, 128), F32)],
        compiler_params=pltpu.CompilerParams(vmem_limit_bytes=12 * 1024 * 1024),
        cost_estimate=pl.CostEstimate(flops=120000000, bytes_accessed=3500000, transcendentals=0),
    )(sums, proj, conv_w)


def pair_block(flags, pair, cot, top, bottom, left, right, rowp, bins, weight):
    chans = 128
    return pl.pallas_call(
        pair_kernel,
        out_shape=(
            jax.ShapeDtypeStruct((32, 64, chans), BF),
            jax.ShapeDtypeStruct((KEPT, chans), F32),
            jax.ShapeDtypeStruct((KEPT, chans), BF),
            jax.ShapeDtypeStruct((40, chans), BF),
        ),
        in_specs=[SMEM] + [VMEM] * 9,
        out_specs=(VMEM,) * 4,
        scratch_shapes=[
            pltpu.VMEM((38, 96, chans), F32),
            pltpu.VMEM((38, WIDE, 3 * chans), BF),
            pltpu.VMEM((36, WIDE, chans), F32),
            pltpu.VMEM((36, 96, chans), F32),
            pltpu.VMEM((36, WIDE, 3 * chans), BF),
            pltpu.VMEM((9 * chans, chans), F32),
            pltpu.VMEM((72, chans), F32),
            pltpu.VMEM((96, chans), F32),
            pltpu.VMEM((9 * chans, chans), BF),
        ],
        compiler_params=pltpu.CompilerParams(vmem_limit_bytes=24 * 1024 * 1024),
        cost_estimate=pl.CostEstimate(flops=2500000000, bytes_accessed=4000000, transcendentals=700000),
    )(flags, pair, cot, top, bottom, left, right, rowp, bins, weight)


def local(fine, conv_w, proj_a, proj_b, pair_in, pair_w, cotangent):
    pairs = pair_in.shape[3]
    row, col = lax.axis_index("row"), lax.axis_index("col")
    core, zpos = row % 2, row // 2
    place = jnp.arange(8)
    place, spot, most = place // 2, jnp.where(place < 2, row, jnp.where(place < 4, col, core)), place % 2
    flags = jnp.where(most == 0, spot > 0, spot < jnp.where(place == 0, 15, 7)).astype(jnp.int32)

    fine, pair, cot = fine[0], pair_in[0], cotangent[0]
    apart = zpos ^ col
    scalars = (core == 0, (apart & 4) == 4, [(apart & 3) == k for k in (1, 2, 3)], zpos == col, [(zpos ^ k) & 3 for k in range(4)])
    edge, flags, scalars = lax.optimization_barrier((fine[-8:], flags, scalars))
    is_first, is_far, is_near, is_root, places = scalars
    before = shift(edge, "row", 1)
    after = shift(fine[:8], "row", -1)
    top = shift(jnp.concatenate([pair[29:], cot[30:]]), "row", 1)
    bottom = shift(jnp.concatenate([pair[:3], cot[:2]]), "row", -1)
    proj = jnp.concatenate([proj_a, proj_b], axis=1)
    part = conv_forward(flags, fine, before, after, conv_w, proj)

    tall_pair = jnp.concatenate([top[:3], pair, bottom[:3]])
    tall_cot = jnp.concatenate([top[2:], cot, bottom[3:], bottom[4:]])
    left = jnp.concatenate([tall_pair[:, 61:], tall_cot[:, 62:], tall_cot[:, :3]], axis=1)
    right = jnp.concatenate([tall_pair[:, :3], tall_cot[:, :5]], axis=1)

    both = up(sum_flip(sum_y(part), "col", 1))
    rowp, colp_here = both[:, :pairs], both[:, pairs:].astype(BF)

    mine = jnp.where(is_first, colp_here[:35], colp_here[3:38])
    other = flip(mine, "row", 1)
    colp = jnp.concatenate([jnp.where(is_first, mine, other), jnp.where(is_first, other, mine)])
    colp, left, right = lax.optimization_barrier((colp, left, right))
    far, left, right = flip(colp, "row", 8), shift(left, "col", 1), shift(right, "col", -1)
    far, left, right = lax.optimization_barrier((far, left, right))
    colp = jnp.where(is_far, far, colp)
    near = [flip(colp, "row", 2 * k) for k in (1, 2, 3)]
    for k in (1, 2, 3):
        colp = jnp.where(is_near[k - 1], near[k - 1], colp)
    weight = pair_w.reshape(9 * pairs, pairs)
    out, keep, send, rowg = pair_block(flags, pair, cot, top, bottom, left, right, rowp, up(colp), weight)

    total = (keep + up(flip(send, "row", 1))).astype(BF)
    half, colg = total[:576].reshape(4, 144, pairs), total[576:]

    def quarter(k):
        return taken(half, places[k])

    def joined(k):
        return jnp.concatenate([quarter(k), colg])

    got = [flip(joined(k), "row", 2 * k) for k in (1, 2, 3)]
    total = ((up(joined(0)) + up(got[0])) + (up(got[1]) + up(got[2]))).astype(BF)
    total = sum_flip(total, "row", 8)
    colg = jnp.where(is_root, total[144:], 0)
    total = sum_y(jnp.concatenate([total[:144], rowg, colg]))
    total = sum_flip(total, "col", 1)
    quart, sums = total[:144], total[144:]
    parts = conv_backward(sums, proj, conv_w)
    quart = sum_flip(quart, "batch", 1)
    parts, quart = lax.optimization_barrier((parts, quart))
    parts = lax.all_to_all(parts, "col", 0, 0, tiled=True)

    near = jnp.stack([quart] + [flip(quart, "row", 2 * k) for k in (1, 2, 3)])
    half = jnp.concatenate([taken(near, places[k]) for k in range(4)])
    theirs = flip(half, "row", 1)
    grad_pair_w = jnp.concatenate([jnp.where(is_first, half, theirs), jnp.where(is_first, theirs, half)])
    grad_pair_w = up(grad_pair_w).reshape(3, 3, pairs, pairs) / 512.0

    grad_fine = jnp.sum(up(parts), axis=0).astype(BF)
    return out[None], grad_fine[None], grad_pair_w


def solution(mesh):
    return jax.shard_map(
        local,
        mesh=mesh,
        in_specs=(
            P("batch", "row", None),
            P(None, "col", None),
            P("col", None),
            P("col", None),
            P("batch", "row", "col", None),
            P(),
            P("batch", "row", "col", None),
        ),
        out_specs=(P("batch", "row", "col", None), P("batch", "row", "col"), P()),
        check_vma=False,
    )
```

```python
import jax
import jax.numpy as jnp
from jax import lax
from jax.experimental import pallas as pl
from jax.experimental.pallas import tpu as pltpu
from jax.sharding import PartitionSpec as P

BF = jnp.bfloat16
F32 = jnp.float32
WIDE = 80
KEPT = 616


def shift(x, axis, step):
    count = lax.axis_size(axis)
    return lax.ppermute(x, axis, [(i, (i + step) % count) for i in range(count)])


def flip(x, axis, bit):
    count = lax.axis_size(axis)
    return lax.ppermute(x, axis, [(i, i ^ bit) for i in range(count)])


def up(x):
    return x.astype(F32)


def sum_y(x):
    across, left, right = shift(x, "col", 4), shift(x, "col", 2), shift(x, "col", 6)
    return ((up(x) + up(across)) + (up(left) + up(right))).astype(BF)


def sum_flip(x, axis, bit):
    return (up(x) + up(flip(x, axis, bit))).astype(BF)


def taken(x, at):
    return lax.dynamic_slice(x, (at, 0, 0), (1,) + x.shape[1:], allow_negative_indices=False)[0]


def pair_kernel(
    flags, pair, cot, top, bottom, halos, rowp, bins, weight, turned,
    out, keep, send, rowg,
    zwide, z3, cots, qwide, q3, wgrad, line, colp, packed, left, right,
):
    chans = 128
    has_up, has_down, has_left, has_right, core = (flags[i] for i in range(5))
    rows = lax.broadcasted_iota(jnp.int32, (38, 1, 1), 0)
    row_ok = ((rows >= 3) | (has_up > 0)) & ((rows < 35) | (has_down > 0))

    colp[...] = jnp.zeros((96, chans), F32)
    colp[5:75] = bins[0:70]
    colp[85:88] = bins[0:3]
    colp[88:89] = bins[3:4]

    packed[...] = up(halos[...])
    for i in range(38):
        left[i, 0:5] = packed[5 * i : 5 * i + 5]
        right[i, 0:5] = packed[192 + 5 * i : 197 + 5 * i]

    zwide[:, 0:8] = jnp.zeros((38, 8, chans), F32)
    zwide[:, 72:96] = jnp.zeros((38, 24, chans), F32)
    cots[:, 64:80] = jnp.zeros((36, 16, chans), F32)

    def zeta(values, first, count, lo, hi):
        scaled = rowp[first : first + count][:, None, :] * colp[lo:hi][None, :, :]
        return up((up(values) + scaled).astype(BF))

    zwide[0:3, 8:72] = jnp.where(has_up > 0, zeta(top[3:6], 0, 3, 8, 72), 0.0)
    zwide[35:38, 8:72] = jnp.where(has_down > 0, zeta(bottom[3:6], 35, 3, 8, 72), 0.0)
    cots[0:2, 0:64] = jnp.where(has_up > 0, up(top[6:8]), 0.0)
    cots[34:36, 0:64] = jnp.where(has_down > 0, up(bottom[6:8]), 0.0)
    edge = jnp.where(row_ok & (has_left > 0), zeta(left[:, 0:3], 0, 38, 5, 8), 0.0)
    zwide[:, 5:8] = edge
    zwide[:, 85:88] = edge
    edge = jnp.where(row_ok & (has_right > 0), zeta(right[:, 0:3], 0, 38, 72, 75), 0.0)
    zwide[:, 72:75] = edge
    cots[:, 78:80] = jnp.where(row_ok[1:37] & (has_left > 0), up(left[1:37, 3:5]), 0.0)
    cots[:, 64:66] = jnp.where(row_ok[1:37] & (has_right > 0), up(right[1:37, 3:5]), 0.0)
    for at in range(0, 32, 4):
        zwide[at + 3 : at + 7, 8:72] = zeta(pair[at : at + 4], at + 3, 4, 8, 72)
        cots[at + 2 : at + 6, 0:64] = up(cot[at : at + 4])
    zwide[:, 88:89] = zwide[:, 8:9]
    for at in range(0, 38, 2):
        for across in range(3):
            z3[at : at + 2, :, across * chans : (across + 1) * chans] = zwide[
                at : at + 2, 7 + across : 87 + across
            ].astype(BF)

    qwide[:, 0:8] = jnp.zeros((36, 8, chans), F32)
    qwide[:, 88:96] = jnp.zeros((36, 8, chans), F32)
    for at in range(0, 36, 6):
        taps = jnp.concatenate([z3[at + d : at + d + 6].reshape(6 * WIDE, 3 * chans) for d in range(3)], axis=1)
        hidden = jnp.dot(taps, weight[...], preferred_element_type=F32).reshape(6, WIDE, chans)
        sigma = jax.nn.sigmoid(hidden)
        grown = hidden * sigma
        q = cots[at : at + 6] * (sigma + grown * (1.0 - sigma))
        qwide[at : at + 6, 8:88] = up(q.astype(BF))
        lo, hi = max(at, 2), min(at + 6, 34)
        out[lo - 2 : hi - 2] = (
            zwide[lo + 1 : hi + 1, 8:72] + grown[lo - at : hi - at, 0:64]
        ).astype(BF)
    qwide[:, 7:8] = qwide[:, 87:88]
    qwide[:, 88:89] = qwide[:, 8:9]
    for at in range(0, 36, 2):
        for across in range(3):
            q3[at : at + 2, :, across * chans : (across + 1) * chans] = qwide[
                at : at + 2, 9 - across : 89 - across
            ].astype(BF)

    own = q3[2:34, 0:64, chans : 2 * chans].reshape(2048, chans)
    for down in range(3):
        near = z3[down + 2 : down + 34, 0:64].reshape(2048, 3 * chans)
        part = lax.dot_general(own, near, (((0,), (0,)), ((), ())), preferred_element_type=F32)
        for across in range(3):
            at = (3 * down + across) * chans
            wgrad[at : at + chans] = part[:, across * chans : (across + 1) * chans].T

    total = jnp.zeros((WIDE, chans), F32)
    rowg[...] = jnp.zeros((40, chans), BF)
    for at in range(0, 34, 6):
        count = min(6, 34 - at)
        taps = jnp.concatenate(
            [q3[at + 2 - d : at + 2 - d + count].reshape(count * WIDE, 3 * chans) for d in range(3)], axis=1
        )
        zgrad = jnp.dot(taps, turned[...], preferred_element_type=F32).reshape(count, WIDE, chans)
        zgrad = zgrad + cots[at + 1 : at + 1 + count]
        rowg[at : at + count] = jnp.sum(zgrad[:, 0:64] * colp[8:72][None], axis=1).astype(BF)
        for i in range(count):
            if 1 <= at + i < 33:
                total = total + zgrad[i] * rowp[at + i + 2 : at + i + 3]
    rowg[0:1] = jnp.where(has_up > 0, rowg[0:1], 0.0)
    rowg[33:34] = jnp.where(has_down > 0, rowg[33:34], 0.0)
    line[0:1] = jnp.where(has_left > 0, total[79:80], 0.0)
    line[1:65] = total[0:64]
    line[65:66] = jnp.where(has_right > 0, total[64:65], 0.0)
    keep[576:616] = jnp.zeros((40, chans), F32)
    send[576:616] = jnp.zeros((40, chans), BF)
    for mine in range(2):

        @pl.when(core == mine)
        def _(mine=mine):
            keep[0:576] = wgrad[576 * mine : 576 * mine + 576]
            send[0:576] = wgrad[576 - 576 * mine : 1152 - 576 * mine].astype(BF)
            keep[576:610] = line[32 * mine : 32 * mine + 34]
            send[576:610] = line[32 - 32 * mine : 66 - 32 * mine].astype(BF)


def run_all(copies):
    for copy in copies:
        copy.start()
    for copy in copies:
        copy.wait()


def turn_kernel(weight, turned):
    for at in range(0, weight.shape[0], 128):
        turned[at : at + 128] = up(weight[at : at + 128]).T.astype(BF)


def begin_kernel(given, taken):
    taken[...] = given[...]


def ends_kernel(fine, pair, cot, begun, to_next, to_last, sems):
    copies = []

    def add(source, target):
        copies.append(pltpu.make_async_copy(source, target, sems.at[len(copies)]))

    blocks = fine.shape[1] // 128
    for ref, spots, pair_rows, cot_rows in ((to_next, 48, 29, 30), (to_last, 0, 0, 0)):
        for j in range(blocks):
            add(fine.at[spots : spots + 16, 128 * j : 128 * j + 128], ref.at[j // 4, 16 * (j % 4) : 16 * (j % 4) + 16])
        add(pair.at[pair_rows : pair_rows + 3], ref.at[3:6])
        add(cot.at[cot_rows : cot_rows + 2], ref.at[6:8])
    run_all(copies)


def conv_kernel(
    flags, fine, top, bottom, conv_w, proj_a, proj_b, pair, cot,
    to_next, to_last, wide, edge,
):
    blocks = wide.shape[0]
    wide[:, 80:88] = jnp.zeros((blocks, 8, 128), F32)
    for j in range(blocks):
        lanes = slice(128 * j, 128 * j + 128)
        spots = up(top[j // 4, 16 * (j % 4) : 16 * (j % 4) + 16])
        wide[j, 0:8] = jnp.where(flags[0] > 0, spots[8:], 0.0)
        wide[j, 8:72] = up(fine[:, lanes])
        spots = up(bottom[j // 4, 16 * (j % 4) : 16 * (j % 4) + 16])
        wide[j, 72:80] = jnp.where(flags[1] > 0, spots[:8], 0.0)
    seq = jnp.zeros((40, conv_w.shape[1]), F32)
    for tap in range(5):
        window = jnp.concatenate([wide[j, pl.ds(tap, 40, stride=2)] for j in range(blocks)], axis=1)
        seq = seq + lax.dot_general(
            window.astype(BF), conv_w[tap], (((1,), (1,)), ((), ())), preferred_element_type=F32
        )
    rows = lax.broadcasted_iota(jnp.int32, (40, 1), 0)
    ok = ((rows >= 3) | (flags[0] > 0)) & ((rows < 35) | (flags[1] > 0)) & (rows < 38)
    seq = jnp.where(ok, seq, 0.0).astype(BF)
    rowp = jnp.dot(seq, proj_a[...], preferred_element_type=F32).astype(BF)
    colp = jnp.dot(seq, proj_b[...], preferred_element_type=F32).astype(BF)
    for ref in (to_next, to_last):
        ref[0:40] = rowp
        ref[40:80] = colp

    edge[...] = jnp.zeros(edge.shape, F32)
    for ref, pair_cols, cot_cols in ((to_next, (61, 64), (62, 64)), (to_last, (0, 3), (0, 2))):
        for i in range(38):
            if i < 3:
                ours, theirs = top[i + 3 : i + 4], top[i + 5 : i + 6]
            elif i < 35:
                ours, theirs = pair[i - 3 : i - 2], cot[i - 3 : i - 2]
            else:
                ours, theirs = bottom[i - 32 : i - 31], bottom[min(i - 29, 7) : min(i - 28, 8)]
            edge[5 * i : 5 * i + 3] = up(ours[0, pair_cols[0] : pair_cols[1]])
            edge[5 * i + 3 : 5 * i + 5] = up(theirs[0, cot_cols[0] : cot_cols[1]])
        ref[80:272] = edge[...].astype(BF)


def grad_conv_kernel(sums, proj_a, proj_b, conv_w, parts, seqg, whole):
    grad = sum(
        lax.dot_general(x, proj[...], (((1,), (1,)), ((), ())), preferred_element_type=F32)
        for x, proj in ((sums[0:40], proj_a), (sums[40:80], proj_b))
    )
    seqg[...] = up(grad.astype(BF))
    ahead, here, behind = (seqg[at : at + 32].astype(BF) for at in (2, 1, 0))

    def times(x, tap):
        return jnp.dot(x, conv_w[tap], preferred_element_type=F32)

    even = times(ahead, 0) + times(here, 2) + times(behind, 4)
    odd = times(ahead, 1) + times(here, 3)
    for j in range(whole.shape[0]):
        lanes = slice(128 * j, 128 * j + 128)
        whole[j, pl.ds(0, 32, stride=2)] = even[:, lanes]
        whole[j, pl.ds(1, 32, stride=2)] = odd[:, lanes]
    for m in range(4):
        low, middle, high = (whole[3 * m + i] for i in range(3))
        parts[2 * m] = jnp.concatenate([low, middle[:, :64]], axis=1).astype(BF)
        parts[2 * m + 1] = jnp.concatenate([middle[:, 64:], high], axis=1).astype(BF)


VMEM = pl.BlockSpec(memory_space=pltpu.VMEM)
SMEM = pl.BlockSpec(memory_space=pltpu.SMEM)


HBM = pl.BlockSpec(memory_space=pltpu.HBM)


def transposed(weight):
    return pl.pallas_call(
        turn_kernel,
        out_shape=jax.ShapeDtypeStruct(weight.shape, BF),
        in_specs=[VMEM],
        out_specs=VMEM,
        compiler_params=pltpu.CompilerParams(vmem_limit_bytes=4 * 1024 * 1024),
        cost_estimate=pl.CostEstimate(flops=40000000000, bytes_accessed=600000, transcendentals=0),
    )(weight)


def begin(seed):
    return pl.pallas_call(
        begin_kernel,
        out_shape=jax.ShapeDtypeStruct(seed.shape, seed.dtype),
        in_specs=[VMEM],
        out_specs=VMEM,
        compiler_params=pltpu.CompilerParams(vmem_limit_bytes=1024 * 1024),
        cost_estimate=pl.CostEstimate(flops=40000000000, bytes_accessed=8192, transcendentals=0),
    )(seed)


def ends(fine, pair, cot, begun):
    payload = jax.ShapeDtypeStruct((8, 64, 128), BF)
    return pl.pallas_call(
        ends_kernel,
        out_shape=(payload, payload),
        in_specs=[VMEM] * 4,
        out_specs=(VMEM, VMEM),
        scratch_shapes=[pltpu.SemaphoreType.DMA((2 * (fine.shape[1] // 128) + 4,))],
        compiler_params=pltpu.CompilerParams(vmem_limit_bytes=6 * 1024 * 1024),
        cost_estimate=pl.CostEstimate(flops=0, bytes_accessed=600000, transcendentals=0),
    )(fine, pair, cot, begun)


def conv_forward(*arrays):
    chans = arrays[1].shape[1]
    payload = jax.ShapeDtypeStruct((272, 128), BF)
    return pl.pallas_call(
        conv_kernel,
        out_shape=(payload, payload),
        in_specs=[SMEM] + [VMEM] * 8,
        out_specs=(VMEM, VMEM),
        scratch_shapes=[pltpu.VMEM((chans // 128, 88, 128), F32), pltpu.VMEM((192, 128), F32)],
        compiler_params=pltpu.CompilerParams(vmem_limit_bytes=12 * 1024 * 1024),
        cost_estimate=pl.CostEstimate(flops=120000000, bytes_accessed=3500000, transcendentals=0),
    )(*arrays)


def conv_backward(sums, proj_a, proj_b, conv_w):
    outchans, chans = conv_w.shape[1:]
    return pl.pallas_call(
        grad_conv_kernel,
        out_shape=jax.ShapeDtypeStruct((8, 64, outchans), BF),
        in_specs=[VMEM] * 4,
        out_specs=VMEM,
        scratch_shapes=[pltpu.VMEM((40, outchans), F32), pltpu.VMEM((chans // 128, 64, 128), F32)],
        compiler_params=pltpu.CompilerParams(vmem_limit_bytes=12 * 1024 * 1024),
        cost_estimate=pl.CostEstimate(flops=120000000, bytes_accessed=3500000, transcendentals=0),
    )(sums, proj_a, proj_b, conv_w)


def pair_block(flags, pair, cot, top, bottom, halos, rowp, bins, weight, turned):
    chans = 128
    return pl.pallas_call(
        pair_kernel,
        out_shape=(
            jax.ShapeDtypeStruct((32, 64, chans), BF),
            jax.ShapeDtypeStruct((KEPT, chans), F32),
            jax.ShapeDtypeStruct((KEPT, chans), BF),
            jax.ShapeDtypeStruct((40, chans), BF),
        ),
        in_specs=[SMEM] + [VMEM] * 9,
        out_specs=(VMEM,) * 4,
        scratch_shapes=[
            pltpu.VMEM((38, 96, chans), F32),
            pltpu.VMEM((38, WIDE, 3 * chans), BF),
            pltpu.VMEM((36, WIDE, chans), F32),
            pltpu.VMEM((36, 96, chans), F32),
            pltpu.VMEM((36, WIDE, 3 * chans), BF),
            pltpu.VMEM((9 * chans, chans), F32),
            pltpu.VMEM((72, chans), F32),
            pltpu.VMEM((96, chans), F32),
            pltpu.VMEM((384, chans), F32),
            pltpu.VMEM((38, 8, chans), F32),
            pltpu.VMEM((38, 8, chans), F32),
        ],
        compiler_params=pltpu.CompilerParams(vmem_limit_bytes=24 * 1024 * 1024),
        cost_estimate=pl.CostEstimate(flops=2500000000, bytes_accessed=4000000, transcendentals=700000),
    )(flags, pair, cot, top, bottom, halos, rowp, bins, weight, turned)


def local(fine, conv_w, proj_a, proj_b, pair_in, pair_w, cotangent):
    pairs = pair_in.shape[3]
    row, col = lax.axis_index("row"), lax.axis_index("col")
    core, zpos = row % 2, row // 2
    place = jnp.arange(8)
    place, spot, most = place // 2, jnp.where(place < 2, row, jnp.where(place < 4, col, core)), place % 2
    flags = jnp.where(most == 0, spot > 0, spot < jnp.where(place == 0, 15, 7)).astype(jnp.int32)

    fine, pair, cot = fine[0], pair_in[0], cotangent[0]
    apart = zpos ^ col
    scalars = (core == 0, (apart & 4) == 4, [(apart & 3) == k for k in (1, 2, 3)], zpos == col, [(zpos ^ k) & 3 for k in range(4)], col % 2 == 1)
    seed, flags, scalars = lax.optimization_barrier((jnp.zeros((8, 128), F32), flags, scalars))
    is_first, is_far, is_near, is_root, places, is_odd = scalars
    down, above = ends(fine, pair, cot, begin(seed))
    top, bottom = shift(down, "row", 1), shift(above, "row", -1)
    weight = pair_w.reshape(9 * pairs, pairs)
    top, bottom, turned = lax.optimization_barrier((top, bottom, transposed(weight)))
    to_next, to_last = conv_forward(flags, fine, top, bottom, conv_w, proj_a, proj_b, pair, cot)

    across, from_last, from_next = shift(to_next[:80], "col", 4), shift(to_next, "col", 2), shift(to_last, "col", -2)
    both = ((up(to_next[:80]) + up(across)) + (up(from_last[:80]) + up(from_next[:80]))).astype(BF)
    to_left = jnp.where(is_odd, from_last[80:], to_next[80:])
    to_right = jnp.where(is_odd, to_last[80:], from_next[80:])
    other = flip(jnp.concatenate([both, to_left, to_right]), "col", 1)
    both, halos = up(both) + up(other[:80]), other[80:]
    rowp, colp_here = both[:40], both[40:].astype(BF)

    mine = jnp.where(is_first, colp_here[:35], colp_here[3:38])
    other = flip(mine, "row", 1)
    colp = jnp.concatenate([jnp.where(is_first, mine, other), jnp.where(is_first, other, mine)])
    colp = jnp.where(is_far, flip(colp, "row", 8), colp)
    near = [flip(colp, "row", 2 * k) for k in (1, 2, 3)]
    for k in (1, 2, 3):
        colp = jnp.where(is_near[k - 1], near[k - 1], colp)
    out, keep, send, rowg = pair_block(flags, pair, cot, top, bottom, halos, rowp, up(colp), weight, turned)

    total = (keep + up(flip(send, "row", 1))).astype(BF)
    half, colg = total[:576].reshape(4, 144, pairs), total[576:]

    def quarter(k):
        return taken(half, places[k])

    def joined(k):
        return jnp.concatenate([quarter(k), colg])

    got = [flip(joined(k), "row", 2 * k) for k in (1, 2, 3)]
    total = ((up(joined(0)) + up(got[0])) + (up(got[1]) + up(got[2]))).astype(BF)
    total = sum_flip(total, "row", 8)
    colg = jnp.where(is_root, total[144:], 0)
    total = sum_y(jnp.concatenate([total[:144], rowg, colg]))
    total = sum_flip(total, "col", 1)
    quart, sums = total[:144], total[144:]
    parts = conv_backward(sums, proj_a, proj_b, conv_w)
    quart = sum_flip(quart, "batch", 1)
    parts, quart = lax.optimization_barrier((parts, quart))
    parts = lax.all_to_all(parts, "col", 0, 0, tiled=True)

    near = jnp.stack([quart] + [flip(quart, "row", 2 * k) for k in (1, 2, 3)])
    half = jnp.concatenate([taken(near, places[k]) for k in range(4)])
    theirs = flip(half, "row", 1)
    grad_pair_w = jnp.concatenate([jnp.where(is_first, half, theirs), jnp.where(is_first, theirs, half)])
    grad_pair_w = up(grad_pair_w).reshape(3, 3, pairs, pairs) / 512.0

    grad_fine = jnp.sum(up(parts), axis=0).astype(BF)
    return out[None], grad_fine[None], grad_pair_w


def solution(mesh):
    return jax.shard_map(
        local,
        mesh=mesh,
        in_specs=(
            P("batch", "row", None),
            P(None, "col", None),
            P("col", None),
            P("col", None),
            P("batch", "row", "col", None),
            P(),
            P("batch", "row", "col", None),
        ),
        out_specs=(P("batch", "row", "col", None), P("batch", "row", "col"), P()),
        check_vma=False,
    )
```

```python
import jax
import jax.numpy as jnp
from jax import lax
from jax.experimental import pallas as pl
from jax.experimental.pallas import tpu as pltpu
from jax.sharding import PartitionSpec as P

BF = jnp.bfloat16
F32 = jnp.float32
WIDE = 80
KEPT = 616


def shift(x, axis, step):
    count = lax.axis_size(axis)
    return lax.ppermute(x, axis, [(i, (i + step) % count) for i in range(count)])


def flip(x, axis, bit):
    count = lax.axis_size(axis)
    return lax.ppermute(x, axis, [(i, i ^ bit) for i in range(count)])


def spread(x, far):
    def place(z, core, col):
        return (z % 8 * 2 + core) * 8 + col

    pairs = {}
    for col in range(8):
        pairs[place(col, 0, col)] = place(col + far, 0, col)
        if far < 4:
            pairs[place(col, 1, col)] = place(col - far, 1, col)
    open_ends = set(range(128)) - set(pairs.values())
    for at in range(128):
        if at not in pairs and at ^ 8 in open_ends:
            pairs[at] = at ^ 8
            open_ends.remove(at ^ 8)
    for at in range(128):
        if at not in pairs:
            pairs[at] = min(end for end in open_ends if end % 8 == at % 8)
            open_ends.remove(pairs[at])
    return lax.ppermute(x, ("row", "col"), sorted(pairs.items()))


def up(x):
    return x.astype(F32)


def sum_y(x):
    across, left, right = shift(x, "col", 4), shift(x, "col", 2), shift(x, "col", 6)
    return ((up(x) + up(across)) + (up(left) + up(right))).astype(BF)


def sum_flip(x, axis, bit):
    return (up(x) + up(flip(x, axis, bit))).astype(BF)


def taken(x, at):
    return lax.dynamic_slice(x, (at, 0, 0), (1,) + x.shape[1:], allow_negative_indices=False)[0]


def pair_kernel(
    flags, pair, cot, top, bottom, halos, rowp, bins, weight, turned,
    out, keep, send, rowg,
    zwide, z3, cots, qwide, q3, wgrad, line, colp, packed, left, right,
):
    chans = 128
    has_up, has_down, has_left, has_right, core = (flags[i] for i in range(5))
    rows = lax.broadcasted_iota(jnp.int32, (38, 1, 1), 0)
    row_ok = ((rows >= 3) | (has_up > 0)) & ((rows < 35) | (has_down > 0))

    colp[...] = jnp.zeros((96, chans), F32)
    colp[5:75] = bins[0:70]
    colp[85:88] = bins[0:3]
    colp[88:89] = bins[3:4]

    packed[...] = up(halos[...])
    for i in range(38):
        left[i, 0:5] = packed[5 * i : 5 * i + 5]
        right[i, 0:5] = packed[192 + 5 * i : 197 + 5 * i]

    zwide[:, 0:8] = jnp.zeros((38, 8, chans), F32)
    zwide[:, 72:96] = jnp.zeros((38, 24, chans), F32)
    cots[:, 64:80] = jnp.zeros((36, 16, chans), F32)

    def zeta(values, first, count, lo, hi):
        scaled = rowp[first : first + count][:, None, :] * colp[lo:hi][None, :, :]
        return up((up(values) + scaled).astype(BF))

    zwide[0:3, 8:72] = jnp.where(has_up > 0, zeta(top[3:6], 0, 3, 8, 72), 0.0)
    zwide[35:38, 8:72] = jnp.where(has_down > 0, zeta(bottom[3:6], 35, 3, 8, 72), 0.0)
    cots[0:2, 0:64] = jnp.where(has_up > 0, up(top[6:8]), 0.0)
    cots[34:36, 0:64] = jnp.where(has_down > 0, up(bottom[6:8]), 0.0)
    edge = jnp.where(row_ok & (has_left > 0), zeta(left[:, 0:3], 0, 38, 5, 8), 0.0)
    zwide[:, 5:8] = edge
    zwide[:, 85:88] = edge
    edge = jnp.where(row_ok & (has_right > 0), zeta(right[:, 0:3], 0, 38, 72, 75), 0.0)
    zwide[:, 72:75] = edge
    cots[:, 78:80] = jnp.where(row_ok[1:37] & (has_left > 0), up(left[1:37, 3:5]), 0.0)
    cots[:, 64:66] = jnp.where(row_ok[1:37] & (has_right > 0), up(right[1:37, 3:5]), 0.0)
    for at in range(0, 32, 4):
        zwide[at + 3 : at + 7, 8:72] = zeta(pair[at : at + 4], at + 3, 4, 8, 72)
        cots[at + 2 : at + 6, 0:64] = up(cot[at : at + 4])
    zwide[:, 88:89] = zwide[:, 8:9]
    for at in range(0, 38, 2):
        for across in range(3):
            z3[at : at + 2, :, across * chans : (across + 1) * chans] = zwide[
                at : at + 2, 7 + across : 87 + across
            ].astype(BF)

    qwide[:, 0:8] = jnp.zeros((36, 8, chans), F32)
    qwide[:, 88:96] = jnp.zeros((36, 8, chans), F32)
    for at in range(0, 36, 6):
        taps = jnp.concatenate([z3[at + d : at + d + 6].reshape(6 * WIDE, 3 * chans) for d in range(3)], axis=1)
        hidden = jnp.dot(taps, weight[...], preferred_element_type=F32).reshape(6, WIDE, chans)
        sigma = jax.nn.sigmoid(hidden)
        grown = hidden * sigma
        q = cots[at : at + 6] * (sigma + grown * (1.0 - sigma))
        qwide[at : at + 6, 8:88] = up(q.astype(BF))
        lo, hi = max(at, 2), min(at + 6, 34)
        out[lo - 2 : hi - 2] = (
            zwide[lo + 1 : hi + 1, 8:72] + grown[lo - at : hi - at, 0:64]
        ).astype(BF)
    qwide[:, 7:8] = qwide[:, 87:88]
    qwide[:, 88:89] = qwide[:, 8:9]
    for at in range(0, 36, 2):
        for across in range(3):
            q3[at : at + 2, :, across * chans : (across + 1) * chans] = qwide[
                at : at + 2, 9 - across : 89 - across
            ].astype(BF)

    own = q3[2:34, 0:64, chans : 2 * chans].reshape(2048, chans)
    for down in range(3):
        near = z3[down + 2 : down + 34, 0:64].reshape(2048, 3 * chans)
        part = lax.dot_general(own, near, (((0,), (0,)), ((), ())), preferred_element_type=F32)
        for across in range(3):
            at = (3 * down + across) * chans
            wgrad[at : at + chans] = part[:, across * chans : (across + 1) * chans].T

    total = jnp.zeros((WIDE, chans), F32)
    rowg[...] = jnp.zeros((40, chans), BF)
    for at in range(0, 34, 6):
        count = min(6, 34 - at)
        taps = jnp.concatenate(
            [q3[at + 2 - d : at + 2 - d + count].reshape(count * WIDE, 3 * chans) for d in range(3)], axis=1
        )
        zgrad = jnp.dot(taps, turned[...], preferred_element_type=F32).reshape(count, WIDE, chans)
        zgrad = zgrad + cots[at + 1 : at + 1 + count]
        rowg[at : at + count] = jnp.sum(zgrad[:, 0:64] * colp[8:72][None], axis=1).astype(BF)
        for i in range(count):
            if 1 <= at + i < 33:
                total = total + zgrad[i] * rowp[at + i + 2 : at + i + 3]
    rowg[0:1] = jnp.where(has_up > 0, rowg[0:1], 0.0)
    rowg[33:34] = jnp.where(has_down > 0, rowg[33:34], 0.0)
    line[0:1] = jnp.where(has_left > 0, total[79:80], 0.0)
    line[1:65] = total[0:64]
    line[65:66] = jnp.where(has_right > 0, total[64:65], 0.0)
    keep[576:616] = jnp.zeros((40, chans), F32)
    send[576:616] = jnp.zeros((40, chans), BF)
    for mine in range(2):

        @pl.when(core == mine)
        def _(mine=mine):
            keep[0:576] = wgrad[576 * mine : 576 * mine + 576]
            send[0:576] = wgrad[576 - 576 * mine : 1152 - 576 * mine].astype(BF)
            keep[576:610] = line[32 * mine : 32 * mine + 34]
            send[576:610] = line[32 - 32 * mine : 66 - 32 * mine].astype(BF)


def run_all(copies):
    for copy in copies:
        copy.start()
    for copy in copies:
        copy.wait()


def turn_kernel(weight, turned):
    for at in range(0, weight.shape[0], 128):
        turned[at : at + 128] = up(weight[at : at + 128]).T.astype(BF)


def begin_kernel(given, taken):
    taken[...] = given[...]


def ends_kernel(fine, pair, cot, begun, to_next, to_last, sems):
    copies = []

    def add(source, target):
        copies.append(pltpu.make_async_copy(source, target, sems.at[len(copies)]))

    blocks = fine.shape[1] // 128
    for ref, spots, pair_rows, cot_rows in ((to_next, 48, 29, 30), (to_last, 0, 0, 0)):
        for j in range(blocks):
            add(fine.at[spots : spots + 16, 128 * j : 128 * j + 128], ref.at[j // 4, 16 * (j % 4) : 16 * (j % 4) + 16])
        add(pair.at[pair_rows : pair_rows + 3], ref.at[3:6])
        add(cot.at[cot_rows : cot_rows + 2], ref.at[6:8])
    run_all(copies)


def conv_kernel(
    flags, fine, top, bottom, conv_w, proj_a, proj_b, pair, cot,
    to_next, to_last, wide, edge,
):
    blocks = wide.shape[0]
    wide[:, 80:88] = jnp.zeros((blocks, 8, 128), F32)
    for j in range(blocks):
        lanes = slice(128 * j, 128 * j + 128)
        spots = up(top[j // 4, 16 * (j % 4) : 16 * (j % 4) + 16])
        wide[j, 0:8] = jnp.where(flags[0] > 0, spots[8:], 0.0)
        wide[j, 8:72] = up(fine[:, lanes])
        spots = up(bottom[j // 4, 16 * (j % 4) : 16 * (j % 4) + 16])
        wide[j, 72:80] = jnp.where(flags[1] > 0, spots[:8], 0.0)
    seq = jnp.zeros((40, conv_w.shape[1]), F32)
    for tap in range(5):
        window = jnp.concatenate([wide[j, pl.ds(tap, 40, stride=2)] for j in range(blocks)], axis=1)
        seq = seq + lax.dot_general(
            window.astype(BF), conv_w[tap], (((1,), (1,)), ((), ())), preferred_element_type=F32
        )
    rows = lax.broadcasted_iota(jnp.int32, (40, 1), 0)
    ok = ((rows >= 3) | (flags[0] > 0)) & ((rows < 35) | (flags[1] > 0)) & (rows < 38)
    seq = jnp.where(ok, seq, 0.0).astype(BF)
    rowp = jnp.dot(seq, proj_a[...], preferred_element_type=F32).astype(BF)
    colp = jnp.dot(seq, proj_b[...], preferred_element_type=F32).astype(BF)
    for ref in (to_next, to_last):
        ref[0:40] = rowp
        ref[40:80] = colp

    edge[...] = jnp.zeros(edge.shape, F32)
    for ref, pair_cols, cot_cols in ((to_next, (61, 64), (62, 64)), (to_last, (0, 3), (0, 2))):
        for i in range(38):
            if i < 3:
                ours, theirs = top[i + 3 : i + 4], top[i + 5 : i + 6]
            elif i < 35:
                ours, theirs = pair[i - 3 : i - 2], cot[i - 3 : i - 2]
            else:
                ours, theirs = bottom[i - 32 : i - 31], bottom[min(i - 29, 7) : min(i - 28, 8)]
            edge[5 * i : 5 * i + 3] = up(ours[0, pair_cols[0] : pair_cols[1]])
            edge[5 * i + 3 : 5 * i + 5] = up(theirs[0, cot_cols[0] : cot_cols[1]])
        ref[80:272] = edge[...].astype(BF)


def grad_conv_kernel(sums, proj_a, proj_b, conv_w, parts, seqg, whole):
    grad = sum(
        lax.dot_general(x, proj[...], (((1,), (1,)), ((), ())), preferred_element_type=F32)
        for x, proj in ((sums[0:40], proj_a), (sums[40:80], proj_b))
    )
    seqg[...] = up(grad.astype(BF))
    ahead, here, behind = (seqg[at : at + 32].astype(BF) for at in (2, 1, 0))

    def times(x, tap):
        return jnp.dot(x, conv_w[tap], preferred_element_type=F32)

    even = times(ahead, 0) + times(here, 2) + times(behind, 4)
    odd = times(ahead, 1) + times(here, 3)
    for j in range(whole.shape[0]):
        lanes = slice(128 * j, 128 * j + 128)
        whole[j, pl.ds(0, 32, stride=2)] = even[:, lanes]
        whole[j, pl.ds(1, 32, stride=2)] = odd[:, lanes]
    for m in range(4):
        low, middle, high = (whole[3 * m + i] for i in range(3))
        parts[2 * m] = jnp.concatenate([low, middle[:, :64]], axis=1).astype(BF)
        parts[2 * m + 1] = jnp.concatenate([middle[:, 64:], high], axis=1).astype(BF)


VMEM = pl.BlockSpec(memory_space=pltpu.VMEM)
SMEM = pl.BlockSpec(memory_space=pltpu.SMEM)


HBM = pl.BlockSpec(memory_space=pltpu.HBM)


def transposed(weight):
    return pl.pallas_call(
        turn_kernel,
        out_shape=jax.ShapeDtypeStruct(weight.shape, BF),
        in_specs=[VMEM],
        out_specs=VMEM,
        compiler_params=pltpu.CompilerParams(vmem_limit_bytes=4 * 1024 * 1024),
        cost_estimate=pl.CostEstimate(flops=40000000000, bytes_accessed=600000, transcendentals=0),
    )(weight)


def begin(seed):
    return pl.pallas_call(
        begin_kernel,
        out_shape=jax.ShapeDtypeStruct(seed.shape, seed.dtype),
        in_specs=[VMEM],
        out_specs=VMEM,
        compiler_params=pltpu.CompilerParams(vmem_limit_bytes=1024 * 1024),
        cost_estimate=pl.CostEstimate(flops=40000000000, bytes_accessed=8192, transcendentals=0),
    )(seed)


def ends(fine, pair, cot, begun):
    payload = jax.ShapeDtypeStruct((8, 64, 128), BF)
    return pl.pallas_call(
        ends_kernel,
        out_shape=(payload, payload),
        in_specs=[VMEM] * 4,
        out_specs=(VMEM, VMEM),
        scratch_shapes=[pltpu.SemaphoreType.DMA((2 * (fine.shape[1] // 128) + 4,))],
        compiler_params=pltpu.CompilerParams(vmem_limit_bytes=6 * 1024 * 1024),
        cost_estimate=pl.CostEstimate(flops=0, bytes_accessed=600000, transcendentals=0),
    )(fine, pair, cot, begun)


def conv_forward(*arrays):
    chans = arrays[1].shape[1]
    payload = jax.ShapeDtypeStruct((272, 128), BF)
    return pl.pallas_call(
        conv_kernel,
        out_shape=(payload, payload),
        in_specs=[SMEM] + [VMEM] * 8,
        out_specs=(VMEM, VMEM),
        scratch_shapes=[pltpu.VMEM((chans // 128, 88, 128), F32), pltpu.VMEM((192, 128), F32)],
        compiler_params=pltpu.CompilerParams(vmem_limit_bytes=12 * 1024 * 1024),
        cost_estimate=pl.CostEstimate(flops=120000000, bytes_accessed=3500000, transcendentals=0),
    )(*arrays)


def conv_backward(sums, proj_a, proj_b, conv_w):
    outchans, chans = conv_w.shape[1:]
    return pl.pallas_call(
        grad_conv_kernel,
        out_shape=jax.ShapeDtypeStruct((8, 64, outchans), BF),
        in_specs=[VMEM] * 4,
        out_specs=VMEM,
        scratch_shapes=[pltpu.VMEM((40, outchans), F32), pltpu.VMEM((chans // 128, 64, 128), F32)],
        compiler_params=pltpu.CompilerParams(vmem_limit_bytes=12 * 1024 * 1024),
        cost_estimate=pl.CostEstimate(flops=120000000, bytes_accessed=3500000, transcendentals=0),
    )(sums, proj_a, proj_b, conv_w)


def pair_block(flags, pair, cot, top, bottom, halos, rowp, bins, weight, turned):
    chans = 128
    return pl.pallas_call(
        pair_kernel,
        out_shape=(
            jax.ShapeDtypeStruct((32, 64, chans), BF),
            jax.ShapeDtypeStruct((KEPT, chans), F32),
            jax.ShapeDtypeStruct((KEPT, chans), BF),
            jax.ShapeDtypeStruct((40, chans), BF),
        ),
        in_specs=[SMEM] + [VMEM] * 9,
        out_specs=(VMEM,) * 4,
        scratch_shapes=[
            pltpu.VMEM((38, 96, chans), F32),
            pltpu.VMEM((38, WIDE, 3 * chans), BF),
            pltpu.VMEM((36, WIDE, chans), F32),
            pltpu.VMEM((36, 96, chans), F32),
            pltpu.VMEM((36, WIDE, 3 * chans), BF),
            pltpu.VMEM((9 * chans, chans), F32),
            pltpu.VMEM((72, chans), F32),
            pltpu.VMEM((96, chans), F32),
            pltpu.VMEM((384, chans), F32),
            pltpu.VMEM((38, 8, chans), F32),
            pltpu.VMEM((38, 8, chans), F32),
        ],
        compiler_params=pltpu.CompilerParams(vmem_limit_bytes=24 * 1024 * 1024),
        cost_estimate=pl.CostEstimate(flops=2500000000, bytes_accessed=4000000, transcendentals=700000),
    )(flags, pair, cot, top, bottom, halos, rowp, bins, weight, turned)


def local(fine, conv_w, proj_a, proj_b, pair_in, pair_w, cotangent):
    pairs = pair_in.shape[3]
    row, col = lax.axis_index("row"), lax.axis_index("col")
    core, zpos = row % 2, row // 2
    place = jnp.arange(8)
    place, spot, most = place // 2, jnp.where(place < 2, row, jnp.where(place < 4, col, core)), place % 2
    flags = jnp.where(most == 0, spot > 0, spot < jnp.where(place == 0, 15, 7)).astype(jnp.int32)

    fine, pair, cot = fine[0], pair_in[0], cotangent[0]
    apart = (zpos - col) & 7
    is_there = [jnp.where(core == 0, apart == far, (apart == 8 - far) & (far < 4)) for far in (1, 2, 3, 4)]
    is_held = (apart == 0) | ((apart <= 4) == (core == 0))
    scalars = (core == 0, is_there, is_held, zpos == col, [(zpos ^ k) & 3 for k in range(4)], col % 2 == 1)
    scalars += ([(col // 2 + k) & 3 for k in range(4)], (zpos & 1) == 1, (zpos & 2) == 2)
    seed, flags, scalars = lax.optimization_barrier((jnp.zeros((8, 128), F32), flags, scalars))
    is_first, is_there, is_held, is_root, places, is_odd, ahead, low_bit, high_bit = scalars
    down, above = ends(fine, pair, cot, begin(seed))
    top, bottom = shift(down, "row", 1), shift(above, "row", -1)
    weight = pair_w.reshape(9 * pairs, pairs)
    top, bottom, turned = lax.optimization_barrier((top, bottom, transposed(weight)))
    to_next, to_last = conv_forward(flags, fine, top, bottom, conv_w, proj_a, proj_b, pair, cot)

    across, from_last, from_next = shift(to_next[:80], "col", 4), shift(to_next, "col", 2), shift(to_last, "col", -2)
    both = ((up(to_next[:80]) + up(across)) + (up(from_last[:80]) + up(from_next[:80]))).astype(BF)
    to_left = jnp.where(is_odd, from_last[80:], to_next[80:])
    to_right = jnp.where(is_odd, to_last[80:], from_next[80:])
    other = flip(jnp.concatenate([both, to_left, to_right]), "col", 1)
    both, halos = up(both) + up(other[:80]), other[80:]
    rowp, colp_here = both[:40], both[40:].astype(BF)

    mine = jnp.where(is_first, colp_here[:35], colp_here[3:38])
    other = flip(mine, "row", 1)
    colp = jnp.concatenate([jnp.where(is_first, mine, other), jnp.where(is_first, other, mine)])
    sent = [spread(colp, far) for far in (4, 3, 2, 1)]
    for far, got in zip((4, 3, 2, 1), sent):
        colp = jnp.where(is_there[far - 1], got, colp)
    colp = jnp.where(is_held, colp, flip(colp, "row", 1))
    out, keep, send, rowg = pair_block(flags, pair, cot, top, bottom, halos, rowp, up(colp), weight, turned)

    total = (keep + up(flip(send, "row", 1))).astype(BF)
    half, colg = total[:576].reshape(4, 144, pairs), total[576:]

    def quarter(k):
        return taken(half, places[k])

    def joined(k):
        return jnp.concatenate([quarter(k), colg])

    got = [flip(joined(k), "row", 2 * k) for k in (1, 2, 3)]
    total = ((up(joined(0)) + up(got[0])) + (up(got[1]) + up(got[2]))).astype(BF)
    total = sum_flip(total, "row", 8)
    colg = jnp.where(is_root, total[144:], 0)
    total = sum_y(jnp.concatenate([total[:144], rowg, colg]))
    total = sum_flip(total, "col", 1)
    quart, sums = total[:144], total[144:]
    parts = conv_backward(sums, proj_a, proj_b, conv_w)
    quart = sum_flip(quart, "batch", 1)
    parts, quart = lax.optimization_barrier((parts, quart))

    parts = parts.reshape(4, 128, parts.shape[2])
    got = [shift(taken(parts, ahead[k]), "col", 2 * k) for k in (1, 2, 3)]
    near = flip(quart, "row", 2)
    got, near = lax.optimization_barrier((got, near))
    mine = (up(taken(parts, ahead[0])) + up(got[0])) + (up(got[1]) + up(got[2]))
    two = jnp.where(low_bit, jnp.concatenate([near, quart]), jnp.concatenate([quart, near]))
    other = flip(jnp.where(is_odd, mine[:64], mine[64:]).astype(BF), "col", 1)
    far = flip(two, "row", 4)
    other, far = lax.optimization_barrier((other, far))
    half = jnp.where(high_bit, jnp.concatenate([far, two]), jnp.concatenate([two, far]))
    theirs = flip(half, "row", 1)
    grad_pair_w = jnp.concatenate([jnp.where(is_first, half, theirs), jnp.where(is_first, theirs, half)])
    grad_pair_w = up(grad_pair_w).reshape(3, 3, pairs, pairs) / 512.0
    grad_fine = (jnp.where(is_odd, mine[64:], mine[:64]) + up(other)).astype(BF)
    return out[None], grad_fine[None], grad_pair_w


def solution(mesh):
    return jax.shard_map(
        local,
        mesh=mesh,
        in_specs=(
            P("batch", "row", None),
            P(None, "col", None),
            P("col", None),
            P("col", None),
            P("batch", "row", "col", None),
            P(),
            P("batch", "row", "col", None),
        ),
        out_specs=(P("batch", "row", "col", None), P("batch", "row", "col"), P()),
        check_vma=False,
    )
```

```python
import jax
import jax.numpy as jnp
from jax import lax
from jax.experimental import pallas as pl
from jax.experimental.pallas import tpu as pltpu
from jax.sharding import PartitionSpec as P

BF = jnp.bfloat16
F32 = jnp.float32
WIDE = 80
STEP = 3
KEPT = 616


def shift(x, axis, step):
    count = lax.axis_size(axis)
    return lax.ppermute(x, axis, [(i, (i + step) % count) for i in range(count)])


def flip(x, axis, bit):
    count = lax.axis_size(axis)
    return lax.ppermute(x, axis, [(i, i ^ bit) for i in range(count)])


def spread(x, far):
    def place(z, core, col):
        return (z % 8 * 2 + core) * 8 + col

    pairs = {}
    for col in range(8):
        pairs[place(col, 0, col)] = place(col + far, 0, col)
        if far < 4:
            pairs[place(col, 1, col)] = place(col - far, 1, col)
    open_ends = set(range(128)) - set(pairs.values())
    for at in range(128):
        if at not in pairs and at ^ 8 in open_ends:
            pairs[at] = at ^ 8
            open_ends.remove(at ^ 8)
    for at in range(128):
        if at not in pairs:
            pairs[at] = min(end for end in open_ends if end % 8 == at % 8)
            open_ends.remove(pairs[at])
    return lax.ppermute(x, ("row", "col"), sorted(pairs.items()))


def up(x):
    return x.astype(F32)


def sum_y(x):
    across, left, right = shift(x, "col", 4), shift(x, "col", 2), shift(x, "col", 6)
    return ((up(x) + up(across)) + (up(left) + up(right))).astype(BF)


def sum_flip(x, axis, bit):
    return (up(x) + up(flip(x, axis, bit))).astype(BF)


def taken(x, at):
    return lax.dynamic_slice(x, (at, 0, 0), (1,) + x.shape[1:], allow_negative_indices=False)[0]


def pair_kernel(
    flags, pair, cot, top, bottom, halos, rowp, bins, ahead, back,
    out, keep, send, rowg,
    zwide, z3, cots, qwide, q3, wgrad, line, colp, packed, left, right,
):
    chans = 128
    has_up, has_down, has_left, has_right, core = (flags[i] for i in range(5))
    rows = lax.broadcasted_iota(jnp.int32, (38, 1, 1), 0)
    row_ok = ((rows >= 3) | (has_up > 0)) & ((rows < 35) | (has_down > 0))

    colp[...] = jnp.zeros((96, chans), F32)
    colp[5:75] = bins[0:70]
    colp[85:88] = bins[0:3]
    colp[88:89] = bins[3:4]

    packed[...] = up(halos[...])
    for i in range(38):
        left[i, 0:5] = packed[5 * i : 5 * i + 5]
        right[i, 0:5] = packed[192 + 5 * i : 197 + 5 * i]

    zwide[:, 0:8] = jnp.zeros((38, 8, chans), F32)
    zwide[:, 72:96] = jnp.zeros((38, 24, chans), F32)
    cots[:, 64:80] = jnp.zeros((36, 16, chans), F32)

    def zeta(values, first, count, lo, hi):
        scaled = rowp[first : first + count][:, None, :] * colp[lo:hi][None, :, :]
        return up((up(values) + scaled).astype(BF))

    zwide[0:3, 8:72] = jnp.where(has_up > 0, zeta(top[3:6], 0, 3, 8, 72), 0.0)
    zwide[35:38, 8:72] = jnp.where(has_down > 0, zeta(bottom[3:6], 35, 3, 8, 72), 0.0)
    cots[0:2, 0:64] = jnp.where(has_up > 0, up(top[6:8]), 0.0)
    cots[34:36, 0:64] = jnp.where(has_down > 0, up(bottom[6:8]), 0.0)
    edge = jnp.where(row_ok & (has_left > 0), zeta(left[:, 0:3], 0, 38, 5, 8), 0.0)
    zwide[:, 5:8] = edge
    zwide[:, 85:88] = edge
    edge = jnp.where(row_ok & (has_right > 0), zeta(right[:, 0:3], 0, 38, 72, 75), 0.0)
    zwide[:, 72:75] = edge
    cots[:, 78:80] = jnp.where(row_ok[1:37] & (has_left > 0), up(left[1:37, 3:5]), 0.0)
    cots[:, 64:66] = jnp.where(row_ok[1:37] & (has_right > 0), up(right[1:37, 3:5]), 0.0)
    for at in range(0, 32, 4):
        zwide[at + 3 : at + 7, 8:72] = zeta(pair[at : at + 4], at + 3, 4, 8, 72)
        cots[at + 2 : at + 6, 0:64] = up(cot[at : at + 4])
    zwide[:, 88:89] = zwide[:, 8:9]
    for at in range(0, 38, 2):
        for across in range(3):
            z3[at : at + 2, :, across * chans : (across + 1) * chans] = zwide[
                at : at + 2, 7 + across : 87 + across
            ].astype(BF)

    qwide[:, 0:8] = jnp.zeros((36, 8, chans), F32)
    qwide[:, 88:96] = jnp.zeros((36, 8, chans), F32)

    def taps(ref, at, count):
        rows = [jnp.concatenate([ref[at + 2 * i + d] for i in range(count)]) for d in range(4)]
        return jnp.concatenate(rows, axis=1)

    for at in range(0, 36, 2 * STEP):
        both = jnp.dot(taps(z3, at, STEP), ahead[...], preferred_element_type=F32)
        for half in range(2):
            for i in range(STEP):
                row = at + 2 * i + half
                hidden = both[i * WIDE : (i + 1) * WIDE, half * chans : (half + 1) * chans]
                sigma = jax.nn.sigmoid(hidden)
                grown = hidden * sigma
                q = cots[row] * (sigma + grown * (1.0 - sigma))
                qwide[row, 8:88] = up(q.astype(BF))
                if 2 <= row < 34:
                    out[row - 2] = (zwide[row + 1, 8:72] + grown[0:64]).astype(BF)
    qwide[:, 7:8] = qwide[:, 87:88]
    qwide[:, 88:89] = qwide[:, 8:9]
    for at in range(0, 36, 2):
        for across in range(3):
            q3[at : at + 2, :, across * chans : (across + 1) * chans] = qwide[
                at : at + 2, 9 - across : 89 - across
            ].astype(BF)

    own = q3[2:34, 0:64, chans : 2 * chans].reshape(2048, chans)
    for down in range(3):
        near = z3[down + 2 : down + 34, 0:64].reshape(2048, 3 * chans)
        part = lax.dot_general(own, near, (((0,), (0,)), ((), ())), preferred_element_type=F32)
        for across in range(3):
            at = (3 * down + across) * chans
            wgrad[at : at + chans] = part[:, across * chans : (across + 1) * chans].T

    total = jnp.zeros((WIDE, chans), F32)
    sums = {}
    for at in range(0, 34, 2 * STEP):
        count = min(STEP, (34 - at) // 2)
        both = jnp.dot(taps(q3, at, count), back[...], preferred_element_type=F32)
        for half in range(2):
            for i in range(count):
                row = at + 2 * i + half
                zgrad = both[i * WIDE : (i + 1) * WIDE, half * chans : (half + 1) * chans] + cots[row + 1]
                sums[row] = jnp.sum(zgrad[0:64] * colp[8:72], axis=0, keepdims=True)
                if 1 <= row < 33:
                    total = total + zgrad * rowp[row + 2 : row + 3]
    sums[0] = jnp.where(has_up > 0, sums[0], 0.0)
    sums[33] = jnp.where(has_down > 0, sums[33], 0.0)
    rowg[...] = jnp.concatenate([sums[row] for row in range(34)] + [jnp.zeros((6, chans), F32)]).astype(BF)
    line[0:1] = jnp.where(has_left > 0, total[79:80], 0.0)
    line[1:65] = total[0:64]
    line[65:66] = jnp.where(has_right > 0, total[64:65], 0.0)
    keep[576:616] = jnp.zeros((40, chans), F32)
    send[576:616] = jnp.zeros((40, chans), BF)
    for mine in range(2):

        @pl.when(core == mine)
        def _(mine=mine):
            keep[0:576] = wgrad[576 * mine : 576 * mine + 576]
            send[0:576] = wgrad[576 - 576 * mine : 1152 - 576 * mine].astype(BF)
            keep[576:610] = line[32 * mine : 32 * mine + 34]
            send[576:610] = line[32 - 32 * mine : 66 - 32 * mine].astype(BF)


def run_all(copies):
    for copy in copies:
        copy.start()
    for copy in copies:
        copy.wait()


def turn_kernel(weight, ahead, back):
    chans = 128
    size = 3 * chans
    for row in range(4):
        here = slice(size * row, size * row + size)
        for out in range(2):
            lanes = slice(chans * out, chans * out + chans)
            tap = row - out
            if 0 <= tap < 3:
                ahead[here, lanes] = weight[size * tap : size * tap + size]
                for across in range(3):
                    at = size * (2 - tap) + chans * across
                    turned = up(weight[at : at + chans]).T.astype(BF)
                    back[size * row + chans * across : size * row + chans * across + chans, lanes] = turned
            else:
                ahead[here, lanes] = jnp.zeros((size, chans), BF)
                back[here, lanes] = jnp.zeros((size, chans), BF)


def begin_kernel(given, taken):
    taken[...] = given[...]


def ends_kernel(fine, pair, cot, begun, to_next, to_last, sems):
    copies = []

    def add(source, target):
        copies.append(pltpu.make_async_copy(source, target, sems.at[len(copies)]))

    blocks = fine.shape[1] // 128
    for ref, spots, pair_rows, cot_rows in ((to_next, 48, 29, 30), (to_last, 0, 0, 0)):
        for j in range(blocks):
            add(fine.at[spots : spots + 16, 128 * j : 128 * j + 128], ref.at[j // 4, 16 * (j % 4) : 16 * (j % 4) + 16])
        add(pair.at[pair_rows : pair_rows + 3], ref.at[3:6])
        add(cot.at[cot_rows : cot_rows + 2], ref.at[6:8])
    run_all(copies)


def conv_kernel(
    flags, fine, top, bottom, conv_w, proj_a, proj_b, pair, cot,
    to_next, to_last, wide, edge,
):
    blocks = wide.shape[0]
    wide[:, 80:88] = jnp.zeros((blocks, 8, 128), F32)
    for j in range(blocks):
        lanes = slice(128 * j, 128 * j + 128)
        spots = up(top[j // 4, 16 * (j % 4) : 16 * (j % 4) + 16])
        wide[j, 0:8] = jnp.where(flags[0] > 0, spots[8:], 0.0)
        wide[j, 8:72] = up(fine[:, lanes])
        spots = up(bottom[j // 4, 16 * (j % 4) : 16 * (j % 4) + 16])
        wide[j, 72:80] = jnp.where(flags[1] > 0, spots[:8], 0.0)
    seq = jnp.zeros((40, conv_w.shape[1]), F32)
    for tap in range(5):
        window = jnp.concatenate([wide[j, pl.ds(tap, 40, stride=2)] for j in range(blocks)], axis=1)
        seq = seq + lax.dot_general(
            window.astype(BF), conv_w[tap], (((1,), (1,)), ((), ())), preferred_element_type=F32
        )
    rows = lax.broadcasted_iota(jnp.int32, (40, 1), 0)
    ok = ((rows >= 3) | (flags[0] > 0)) & ((rows < 35) | (flags[1] > 0)) & (rows < 38)
    seq = jnp.where(ok, seq, 0.0).astype(BF)
    rowp = jnp.dot(seq, proj_a[...], preferred_element_type=F32).astype(BF)
    colp = jnp.dot(seq, proj_b[...], preferred_element_type=F32).astype(BF)
    for ref in (to_next, to_last):
        ref[0:40] = rowp
        ref[40:80] = colp

    edge[...] = jnp.zeros(edge.shape, F32)
    for ref, pair_cols, cot_cols in ((to_next, (61, 64), (62, 64)), (to_last, (0, 3), (0, 2))):
        for i in range(38):
            if i < 3:
                ours, theirs = top[i + 3 : i + 4], top[i + 5 : i + 6]
            elif i < 35:
                ours, theirs = pair[i - 3 : i - 2], cot[i - 3 : i - 2]
            else:
                ours, theirs = bottom[i - 32 : i - 31], bottom[min(i - 29, 7) : min(i - 28, 8)]
            edge[5 * i : 5 * i + 3] = up(ours[0, pair_cols[0] : pair_cols[1]])
            edge[5 * i + 3 : 5 * i + 5] = up(theirs[0, cot_cols[0] : cot_cols[1]])
        ref[80:272] = edge[...].astype(BF)


def grad_conv_kernel(sums, proj_a, proj_b, conv_w, parts, seqg, whole):
    grad = sum(
        lax.dot_general(x, proj[...], (((1,), (1,)), ((), ())), preferred_element_type=F32)
        for x, proj in ((sums[0:40], proj_a), (sums[40:80], proj_b))
    )
    seqg[...] = up(grad.astype(BF))
    ahead, here, behind = (seqg[at : at + 32].astype(BF) for at in (2, 1, 0))

    def times(x, tap):
        return jnp.dot(x, conv_w[tap], preferred_element_type=F32)

    even = times(ahead, 0) + times(here, 2) + times(behind, 4)
    odd = times(ahead, 1) + times(here, 3)
    for j in range(whole.shape[0]):
        lanes = slice(128 * j, 128 * j + 128)
        whole[j, pl.ds(0, 32, stride=2)] = even[:, lanes]
        whole[j, pl.ds(1, 32, stride=2)] = odd[:, lanes]
    for m in range(4):
        low, middle, high = (whole[3 * m + i] for i in range(3))
        parts[2 * m] = jnp.concatenate([low, middle[:, :64]], axis=1).astype(BF)
        parts[2 * m + 1] = jnp.concatenate([middle[:, 64:], high], axis=1).astype(BF)


VMEM = pl.BlockSpec(memory_space=pltpu.VMEM)
SMEM = pl.BlockSpec(memory_space=pltpu.SMEM)


HBM = pl.BlockSpec(memory_space=pltpu.HBM)


def two_row_weights(weight):
    shape = jax.ShapeDtypeStruct((12 * weight.shape[1], 2 * weight.shape[1]), BF)
    return pl.pallas_call(
        turn_kernel,
        out_shape=(shape, shape),
        in_specs=[VMEM],
        out_specs=(VMEM, VMEM),
        compiler_params=pltpu.CompilerParams(vmem_limit_bytes=6 * 1024 * 1024),
        cost_estimate=pl.CostEstimate(flops=40000000000, bytes_accessed=600000, transcendentals=0),
    )(weight)


def begin(seed):
    return pl.pallas_call(
        begin_kernel,
        out_shape=jax.ShapeDtypeStruct(seed.shape, seed.dtype),
        in_specs=[VMEM],
        out_specs=VMEM,
        compiler_params=pltpu.CompilerParams(vmem_limit_bytes=1024 * 1024),
        cost_estimate=pl.CostEstimate(flops=40000000000, bytes_accessed=8192, transcendentals=0),
    )(seed)


def ends(fine, pair, cot, begun):
    payload = jax.ShapeDtypeStruct((8, 64, 128), BF)
    return pl.pallas_call(
        ends_kernel,
        out_shape=(payload, payload),
        in_specs=[VMEM] * 4,
        out_specs=(VMEM, VMEM),
        scratch_shapes=[pltpu.SemaphoreType.DMA((2 * (fine.shape[1] // 128) + 4,))],
        compiler_params=pltpu.CompilerParams(vmem_limit_bytes=6 * 1024 * 1024),
        cost_estimate=pl.CostEstimate(flops=0, bytes_accessed=600000, transcendentals=0),
    )(fine, pair, cot, begun)


def conv_forward(*arrays):
    chans = arrays[1].shape[1]
    payload = jax.ShapeDtypeStruct((272, 128), BF)
    return pl.pallas_call(
        conv_kernel,
        out_shape=(payload, payload),
        in_specs=[SMEM] + [VMEM] * 8,
        out_specs=(VMEM, VMEM),
        scratch_shapes=[pltpu.VMEM((chans // 128, 88, 128), F32), pltpu.VMEM((192, 128), F32)],
        compiler_params=pltpu.CompilerParams(vmem_limit_bytes=12 * 1024 * 1024),
        cost_estimate=pl.CostEstimate(flops=120000000, bytes_accessed=3500000, transcendentals=0),
    )(*arrays)


def conv_backward(sums, proj_a, proj_b, conv_w):
    outchans, chans = conv_w.shape[1:]
    return pl.pallas_call(
        grad_conv_kernel,
        out_shape=jax.ShapeDtypeStruct((8, 64, outchans), BF),
        in_specs=[VMEM] * 4,
        out_specs=VMEM,
        scratch_shapes=[pltpu.VMEM((40, outchans), F32), pltpu.VMEM((chans // 128, 64, 128), F32)],
        compiler_params=pltpu.CompilerParams(vmem_limit_bytes=12 * 1024 * 1024),
        cost_estimate=pl.CostEstimate(flops=120000000, bytes_accessed=3500000, transcendentals=0),
    )(sums, proj_a, proj_b, conv_w)


def pair_block(flags, pair, cot, top, bottom, halos, rowp, bins, ahead, back):
    chans = 128
    return pl.pallas_call(
        pair_kernel,
        out_shape=(
            jax.ShapeDtypeStruct((32, 64, chans), BF),
            jax.ShapeDtypeStruct((KEPT, chans), F32),
            jax.ShapeDtypeStruct((KEPT, chans), BF),
            jax.ShapeDtypeStruct((40, chans), BF),
        ),
        in_specs=[SMEM] + [VMEM] * 9,
        out_specs=(VMEM,) * 4,
        scratch_shapes=[
            pltpu.VMEM((38, 96, chans), F32),
            pltpu.VMEM((38, WIDE, 3 * chans), BF),
            pltpu.VMEM((36, WIDE, chans), F32),
            pltpu.VMEM((36, 96, chans), F32),
            pltpu.VMEM((36, WIDE, 3 * chans), BF),
            pltpu.VMEM((9 * chans, chans), F32),
            pltpu.VMEM((72, chans), F32),
            pltpu.VMEM((96, chans), F32),
            pltpu.VMEM((384, chans), F32),
            pltpu.VMEM((38, 8, chans), F32),
            pltpu.VMEM((38, 8, chans), F32),
        ],
        compiler_params=pltpu.CompilerParams(vmem_limit_bytes=24 * 1024 * 1024),
        cost_estimate=pl.CostEstimate(flops=2500000000, bytes_accessed=4000000, transcendentals=700000),
    )(flags, pair, cot, top, bottom, halos, rowp, bins, ahead, back)


def local(fine, conv_w, proj_a, proj_b, pair_in, pair_w, cotangent):
    pairs = pair_in.shape[3]
    row, col = lax.axis_index("row"), lax.axis_index("col")
    core, zpos = row % 2, row // 2
    place = jnp.arange(8)
    place, spot, most = place // 2, jnp.where(place < 2, row, jnp.where(place < 4, col, core)), place % 2
    flags = jnp.where(most == 0, spot > 0, spot < jnp.where(place == 0, 15, 7)).astype(jnp.int32)

    fine, pair, cot = fine[0], pair_in[0], cotangent[0]
    apart = (zpos - col) & 7
    is_there = [jnp.where(core == 0, apart == far, (apart == 8 - far) & (far < 4)) for far in (1, 2, 3, 4)]
    is_held = (apart == 0) | ((apart <= 4) == (core == 0))
    scalars = (core == 0, is_there, is_held, zpos == col, [(zpos ^ k) & 3 for k in range(4)], col % 2 == 1)
    scalars += ([(col // 2 + k) & 3 for k in range(4)],)
    seed, flags, scalars = lax.optimization_barrier((jnp.zeros((8, 128), F32), flags, scalars))
    is_first, is_there, is_held, is_root, places, is_odd, ahead = scalars
    down, above = ends(fine, pair, cot, begin(seed))
    top, bottom = shift(down, "row", 1), shift(above, "row", -1)
    weight = pair_w.reshape(9 * pairs, pairs)
    top, bottom, weights = lax.optimization_barrier((top, bottom, two_row_weights(weight)))
    to_next, to_last = conv_forward(flags, fine, top, bottom, conv_w, proj_a, proj_b, pair, cot)

    across, from_last, from_next = shift(to_next[:80], "col", 4), shift(to_next, "col", 2), shift(to_last, "col", -2)
    both = ((up(to_next[:80]) + up(across)) + (up(from_last[:80]) + up(from_next[:80]))).astype(BF)
    to_left = jnp.where(is_odd, from_last[80:], to_next[80:])
    to_right = jnp.where(is_odd, to_last[80:], from_next[80:])
    other = flip(jnp.concatenate([both, to_left, to_right]), "col", 1)
    both, halos = up(both) + up(other[:80]), other[80:]
    rowp, colp_here = both[:40], both[40:].astype(BF)

    mine = jnp.where(is_first, colp_here[:35], colp_here[3:38])
    other = flip(mine, "row", 1)
    colp = jnp.concatenate([jnp.where(is_first, mine, other), jnp.where(is_first, other, mine)])
    sent = [spread(colp, far) for far in (4, 3, 2, 1)]
    for far, got in zip((4, 3, 2, 1), sent):
        colp = jnp.where(is_there[far - 1], got, colp)
    colp = jnp.where(is_held, colp, flip(colp, "row", 1))
    out, keep, send, rowg = pair_block(flags, pair, cot, top, bottom, halos, rowp, up(colp), *weights)

    total = (keep + up(flip(send, "row", 1))).astype(BF)
    half, colg = total[:576].reshape(4, 144, pairs), total[576:]

    def quarter(k):
        return taken(half, places[k])

    def joined(k):
        return jnp.concatenate([quarter(k), colg])

    got = [flip(joined(k), "row", 2 * k) for k in (1, 2, 3)]
    total = ((up(joined(0)) + up(got[0])) + (up(got[1]) + up(got[2]))).astype(BF)
    total = sum_flip(total, "row", 8)
    colg = jnp.where(is_root, total[144:], 0)
    total = sum_y(jnp.concatenate([total[:144], rowg, colg]))

    quart = total[:144]
    across, others = flip(total, "col", 1), flip(quart, "batch", 1)
    crossed = lax.ppermute(quart, ("col", "batch"), [(i, i ^ 3) for i in range(16)])
    sums = (up(total[144:]) + up(across[144:])).astype(BF)
    parts = conv_backward(sums, proj_a, proj_b, conv_w)
    quart = ((up(quart) + up(across[:144])) + (up(others) + up(crossed))).astype(BF)
    parts, quart = lax.optimization_barrier((parts, quart))

    parts = parts.reshape(4, 128, parts.shape[2])
    got = [shift(taken(parts, ahead[k]), "col", 2 * k) for k in (1, 2, 3)]
    near = [flip(quart, "row", 2 * k) for k in (1, 2, 3)]
    got, near = lax.optimization_barrier((got, near))
    mine = (up(taken(parts, ahead[0])) + up(got[0])) + (up(got[1]) + up(got[2]))
    near = jnp.stack([quart] + near)
    half = jnp.concatenate([taken(near, places[k]) for k in range(4)])
    other = flip(jnp.where(is_odd, mine[:64], mine[64:]).astype(BF), "col", 1)
    theirs = flip(half, "row", 1)
    grad_pair_w = jnp.concatenate([jnp.where(is_first, half, theirs), jnp.where(is_first, theirs, half)])
    grad_pair_w = up(grad_pair_w).reshape(3, 3, pairs, pairs) / 512.0
    grad_fine = (jnp.where(is_odd, mine[64:], mine[:64]) + up(other)).astype(BF)
    return out[None], grad_fine[None], grad_pair_w


def solution(mesh):
    return jax.shard_map(
        local,
        mesh=mesh,
        in_specs=(
            P("batch", "row", None),
            P(None, "col", None),
            P("col", None),
            P("col", None),
            P("batch", "row", "col", None),
            P(),
            P("batch", "row", "col", None),
        ),
        out_specs=(P("batch", "row", "col", None), P("batch", "row", "col"), P()),
        check_vma=False,
    )
```

```python
import jax
import jax.numpy as jnp
from jax import lax
from jax.experimental import pallas as pl
from jax.experimental.pallas import tpu as pltpu
from jax.sharding import PartitionSpec as P

BF = jnp.bfloat16
F32 = jnp.float32
WIDE = 80
STEP = 3
KEPT = 616


def shift(x, axis, step):
    count = lax.axis_size(axis)
    return lax.ppermute(x, axis, [(i, (i + step) % count) for i in range(count)])


def flip(x, axis, bit):
    count = lax.axis_size(axis)
    return lax.ppermute(x, axis, [(i, i ^ bit) for i in range(count)])


def spread(x, far):
    def place(z, core, col):
        return (z % 8 * 2 + core) * 8 + col

    pairs = {}
    for col in range(8):
        pairs[place(col, 0, col)] = place(col + far, 0, col)
        if far < 4:
            pairs[place(col, 1, col)] = place(col - far, 1, col)
    open_ends = set(range(128)) - set(pairs.values())
    for at in range(128):
        if at not in pairs and at ^ 8 in open_ends:
            pairs[at] = at ^ 8
            open_ends.remove(at ^ 8)
    for at in range(128):
        if at not in pairs:
            pairs[at] = min(end for end in open_ends if end % 8 == at % 8)
            open_ends.remove(pairs[at])
    return lax.ppermute(x, ("row", "col"), sorted(pairs.items()))


def up(x):
    return x.astype(F32)


def sum_y(x):
    across, left, right = shift(x, "col", 4), shift(x, "col", 2), shift(x, "col", 6)
    return ((up(x) + up(across)) + (up(left) + up(right))).astype(BF)


def sum_flip(x, axis, bit):
    return (up(x) + up(flip(x, axis, bit))).astype(BF)


def taken(x, at):
    return lax.dynamic_slice(x, (at, 0, 0), (1,) + x.shape[1:], allow_negative_indices=False)[0]


def pair_kernel(
    flags, pair, cot, top, bottom, halos, rowp, bins, ahead, back,
    out, keep, send, rowg,
    zwide, z3, cots, qwide, q3, wgrad, line, colp, packed, left, right,
):
    chans = 128
    has_up, has_down, has_left, has_right, core = (flags[i] for i in range(5))
    rows = lax.broadcasted_iota(jnp.int32, (38, 1, 1), 0)
    row_ok = ((rows >= 3) | (has_up > 0)) & ((rows < 35) | (has_down > 0))

    colp[...] = jnp.zeros((96, chans), F32)
    colp[5:75] = bins[0:70]
    colp[85:88] = bins[0:3]
    colp[88:89] = bins[3:4]

    packed[...] = up(halos[...])
    for i in range(38):
        left[i, 0:5] = packed[5 * i : 5 * i + 5]
        right[i, 0:5] = packed[192 + 5 * i : 197 + 5 * i]

    zwide[:, 0:8] = jnp.zeros((38, 8, chans), F32)
    zwide[:, 72:96] = jnp.zeros((38, 24, chans), F32)
    cots[:, 64:80] = jnp.zeros((36, 16, chans), F32)

    def zeta(values, first, count, lo, hi):
        scaled = rowp[first : first + count][:, None, :] * colp[lo:hi][None, :, :]
        return up((up(values) + scaled).astype(BF))

    zwide[0:3, 8:72] = jnp.where(has_up > 0, zeta(top[3:6], 0, 3, 8, 72), 0.0)
    zwide[35:38, 8:72] = jnp.where(has_down > 0, zeta(bottom[3:6], 35, 3, 8, 72), 0.0)
    cots[0:2, 0:64] = jnp.where(has_up > 0, up(top[6:8]), 0.0)
    cots[34:36, 0:64] = jnp.where(has_down > 0, up(bottom[6:8]), 0.0)
    edge = jnp.where(row_ok & (has_left > 0), zeta(left[:, 0:3], 0, 38, 5, 8), 0.0)
    zwide[:, 5:8] = edge
    zwide[:, 85:88] = edge
    edge = jnp.where(row_ok & (has_right > 0), zeta(right[:, 0:3], 0, 38, 72, 75), 0.0)
    zwide[:, 72:75] = edge
    cots[:, 78:80] = jnp.where(row_ok[1:37] & (has_left > 0), up(left[1:37, 3:5]), 0.0)
    cots[:, 64:66] = jnp.where(row_ok[1:37] & (has_right > 0), up(right[1:37, 3:5]), 0.0)
    for at in range(0, 32, 4):
        zwide[at + 3 : at + 7, 8:72] = zeta(pair[at : at + 4], at + 3, 4, 8, 72)
        cots[at + 2 : at + 6, 0:64] = up(cot[at : at + 4])
    zwide[:, 88:89] = zwide[:, 8:9]
    for at in range(0, 38, 2):
        for across in range(3):
            z3[at : at + 2, :, across * chans : (across + 1) * chans] = zwide[
                at : at + 2, 7 + across : 87 + across
            ].astype(BF)

    qwide[:, 0:8] = jnp.zeros((36, 8, chans), F32)
    qwide[:, 88:96] = jnp.zeros((36, 8, chans), F32)

    def taps(ref, at, count):
        rows = [jnp.concatenate([ref[at + 2 * i + d] for i in range(count)]) for d in range(4)]
        return jnp.concatenate(rows, axis=1)

    for at in range(0, 36, 2 * STEP):
        both = jnp.dot(taps(z3, at, STEP), ahead[...], preferred_element_type=F32)
        for half in range(2):
            for i in range(STEP):
                row = at + 2 * i + half
                hidden = both[i * WIDE : (i + 1) * WIDE, half * chans : (half + 1) * chans]
                sigma = jax.nn.sigmoid(hidden)
                grown = hidden * sigma
                q = cots[row] * (sigma + grown * (1.0 - sigma))
                qwide[row, 8:88] = up(q.astype(BF))
                if 2 <= row < 34:
                    out[row - 2] = (zwide[row + 1, 8:72] + grown[0:64]).astype(BF)
    qwide[:, 7:8] = qwide[:, 87:88]
    qwide[:, 88:89] = qwide[:, 8:9]
    for at in range(0, 36, 2):
        for across in range(3):
            q3[at : at + 2, :, across * chans : (across + 1) * chans] = qwide[
                at : at + 2, 9 - across : 89 - across
            ].astype(BF)

    own = q3[2:34, 0:64, chans : 2 * chans].reshape(2048, chans)
    for down in range(3):
        near = z3[down + 2 : down + 34, 0:64].reshape(2048, 3 * chans)
        part = lax.dot_general(own, near, (((0,), (0,)), ((), ())), preferred_element_type=F32)
        for across in range(3):
            at = (3 * down + across) * chans
            wgrad[at : at + chans] = part[:, across * chans : (across + 1) * chans].T

    total = jnp.zeros((WIDE, chans), F32)
    sums = {}
    for at in range(0, 34, 2 * STEP):
        count = min(STEP, (34 - at) // 2)
        both = jnp.dot(taps(q3, at, count), back[...], preferred_element_type=F32)
        for half in range(2):
            for i in range(count):
                row = at + 2 * i + half
                zgrad = both[i * WIDE : (i + 1) * WIDE, half * chans : (half + 1) * chans] + cots[row + 1]
                sums[row] = jnp.sum(zgrad[0:64] * colp[8:72], axis=0, keepdims=True)
                if 1 <= row < 33:
                    total = total + zgrad * rowp[row + 2 : row + 3]
    sums[0] = jnp.where(has_up > 0, sums[0], 0.0)
    sums[33] = jnp.where(has_down > 0, sums[33], 0.0)
    rowg[...] = jnp.concatenate([sums[row] for row in range(34)] + [jnp.zeros((6, chans), F32)]).astype(BF)
    line[0:1] = jnp.where(has_left > 0, total[79:80], 0.0)
    line[1:65] = total[0:64]
    line[65:66] = jnp.where(has_right > 0, total[64:65], 0.0)
    keep[576:616] = jnp.zeros((40, chans), F32)
    send[576:616] = jnp.zeros((40, chans), BF)
    for mine in range(2):

        @pl.when(core == mine)
        def _(mine=mine):
            keep[0:576] = wgrad[576 * mine : 576 * mine + 576]
            send[0:576] = wgrad[576 - 576 * mine : 1152 - 576 * mine].astype(BF)
            keep[576:610] = line[32 * mine : 32 * mine + 34]
            send[576:610] = line[32 - 32 * mine : 66 - 32 * mine].astype(BF)


def run_all(copies):
    for copy in copies:
        copy.start()
    for copy in copies:
        copy.wait()


def turn_kernel(weight, ahead, back):
    chans = 128
    size = 3 * chans
    for row in range(4):
        here = slice(size * row, size * row + size)
        for out in range(2):
            lanes = slice(chans * out, chans * out + chans)
            tap = row - out
            if 0 <= tap < 3:
                ahead[here, lanes] = weight[size * tap : size * tap + size]
                for across in range(3):
                    at = size * (2 - tap) + chans * across
                    turned = up(weight[at : at + chans]).T.astype(BF)
                    back[size * row + chans * across : size * row + chans * across + chans, lanes] = turned
            else:
                ahead[here, lanes] = jnp.zeros((size, chans), BF)
                back[here, lanes] = jnp.zeros((size, chans), BF)


def begin_kernel(given, taken):
    taken[...] = given[...]


def ends_kernel(fine, pair, cot, begun, to_next, to_last, sems):
    copies = []

    def add(source, target):
        copies.append(pltpu.make_async_copy(source, target, sems.at[len(copies)]))

    blocks = fine.shape[1] // 128
    for ref, spots, pair_rows, cot_rows in ((to_next, 48, 29, 30), (to_last, 0, 0, 0)):
        for j in range(blocks):
            add(fine.at[spots : spots + 16, 128 * j : 128 * j + 128], ref.at[j // 4, 16 * (j % 4) : 16 * (j % 4) + 16])
        add(pair.at[pair_rows : pair_rows + 3], ref.at[3:6])
        add(cot.at[cot_rows : cot_rows + 2], ref.at[6:8])
    run_all(copies)


def conv_kernel(
    flags, fine, top, bottom, conv_w, proj_a, proj_b, pair, cot,
    to_next, to_last, wide, edge,
):
    blocks = wide.shape[0]
    wide[:, 80:88] = jnp.zeros((blocks, 8, 128), F32)
    for j in range(blocks):
        lanes = slice(128 * j, 128 * j + 128)
        spots = up(top[j // 4, 16 * (j % 4) : 16 * (j % 4) + 16])
        wide[j, 0:8] = jnp.where(flags[0] > 0, spots[8:], 0.0)
        wide[j, 8:72] = up(fine[:, lanes])
        spots = up(bottom[j // 4, 16 * (j % 4) : 16 * (j % 4) + 16])
        wide[j, 72:80] = jnp.where(flags[1] > 0, spots[:8], 0.0)
    seq = jnp.zeros((40, conv_w.shape[1]), F32)
    for tap in range(5):
        window = jnp.concatenate([wide[j, pl.ds(tap, 40, stride=2)] for j in range(blocks)], axis=1)
        seq = seq + lax.dot_general(
            window.astype(BF), conv_w[tap], (((1,), (1,)), ((), ())), preferred_element_type=F32
        )
    rows = lax.broadcasted_iota(jnp.int32, (40, 1), 0)
    ok = ((rows >= 3) | (flags[0] > 0)) & ((rows < 35) | (flags[1] > 0)) & (rows < 38)
    seq = jnp.where(ok, seq, 0.0).astype(BF)
    rowp = jnp.dot(seq, proj_a[...], preferred_element_type=F32).astype(BF)
    colp = jnp.dot(seq, proj_b[...], preferred_element_type=F32).astype(BF)
    for ref in (to_next, to_last):
        ref[0:40] = rowp
        ref[40:80] = colp

    edge[...] = jnp.zeros(edge.shape, F32)
    for ref, pair_cols, cot_cols in ((to_next, (61, 64), (62, 64)), (to_last, (0, 3), (0, 2))):
        for i in range(38):
            if i < 3:
                ours, theirs = top[i + 3 : i + 4], top[i + 5 : i + 6]
            elif i < 35:
                ours, theirs = pair[i - 3 : i - 2], cot[i - 3 : i - 2]
            else:
                ours, theirs = bottom[i - 32 : i - 31], bottom[min(i - 29, 7) : min(i - 28, 8)]
            edge[5 * i : 5 * i + 3] = up(ours[0, pair_cols[0] : pair_cols[1]])
            edge[5 * i + 3 : 5 * i + 5] = up(theirs[0, cot_cols[0] : cot_cols[1]])
        ref[80:272] = edge[...].astype(BF)


def grad_conv_kernel(sums, proj_a, proj_b, conv_w, parts, seqg, whole):
    grad = sum(
        lax.dot_general(x, proj[...], (((1,), (1,)), ((), ())), preferred_element_type=F32)
        for x, proj in ((sums[0:40], proj_a), (sums[40:80], proj_b))
    )
    seqg[...] = up(grad.astype(BF))
    ahead, here, behind = (seqg[at : at + 32].astype(BF) for at in (2, 1, 0))

    def times(x, tap):
        return jnp.dot(x, conv_w[tap], preferred_element_type=F32)

    even = times(ahead, 0) + times(here, 2) + times(behind, 4)
    odd = times(ahead, 1) + times(here, 3)
    for j in range(whole.shape[0]):
        lanes = slice(128 * j, 128 * j + 128)
        whole[j, pl.ds(0, 32, stride=2)] = even[:, lanes]
        whole[j, pl.ds(1, 32, stride=2)] = odd[:, lanes]
    for m in range(4):
        low, middle, high = (whole[3 * m + i] for i in range(3))
        parts[2 * m] = jnp.concatenate([low, middle[:, :64]], axis=1).astype(BF)
        parts[2 * m + 1] = jnp.concatenate([middle[:, 64:], high], axis=1).astype(BF)


VMEM = pl.BlockSpec(memory_space=pltpu.VMEM)
SMEM = pl.BlockSpec(memory_space=pltpu.SMEM)


HBM = pl.BlockSpec(memory_space=pltpu.HBM)


def two_row_weights(weight):
    shape = jax.ShapeDtypeStruct((12 * weight.shape[1], 2 * weight.shape[1]), BF)
    return pl.pallas_call(
        turn_kernel,
        out_shape=(shape, shape),
        in_specs=[VMEM],
        out_specs=(VMEM, VMEM),
        compiler_params=pltpu.CompilerParams(vmem_limit_bytes=6 * 1024 * 1024),
        cost_estimate=pl.CostEstimate(flops=40000000000, bytes_accessed=600000, transcendentals=0),
    )(weight)


def begin(seed):
    return pl.pallas_call(
        begin_kernel,
        out_shape=jax.ShapeDtypeStruct(seed.shape, seed.dtype),
        in_specs=[VMEM],
        out_specs=VMEM,
        compiler_params=pltpu.CompilerParams(vmem_limit_bytes=1024 * 1024),
        cost_estimate=pl.CostEstimate(flops=40000000000, bytes_accessed=8192, transcendentals=0),
    )(seed)


def ends(fine, pair, cot, begun):
    payload = jax.ShapeDtypeStruct((8, 64, 128), BF)
    return pl.pallas_call(
        ends_kernel,
        out_shape=(payload, payload),
        in_specs=[VMEM] * 4,
        out_specs=(VMEM, VMEM),
        scratch_shapes=[pltpu.SemaphoreType.DMA((2 * (fine.shape[1] // 128) + 4,))],
        compiler_params=pltpu.CompilerParams(vmem_limit_bytes=6 * 1024 * 1024),
        cost_estimate=pl.CostEstimate(flops=0, bytes_accessed=600000, transcendentals=0),
    )(fine, pair, cot, begun)


def conv_forward(*arrays):
    chans = arrays[1].shape[1]
    payload = jax.ShapeDtypeStruct((272, 128), BF)
    return pl.pallas_call(
        conv_kernel,
        out_shape=(payload, payload),
        in_specs=[SMEM] + [VMEM] * 8,
        out_specs=(VMEM, VMEM),
        scratch_shapes=[pltpu.VMEM((chans // 128, 88, 128), F32), pltpu.VMEM((192, 128), F32)],
        compiler_params=pltpu.CompilerParams(vmem_limit_bytes=12 * 1024 * 1024),
        cost_estimate=pl.CostEstimate(flops=120000000, bytes_accessed=3500000, transcendentals=0),
    )(*arrays)


def conv_backward(sums, proj_a, proj_b, conv_w):
    outchans, chans = conv_w.shape[1:]
    return pl.pallas_call(
        grad_conv_kernel,
        out_shape=jax.ShapeDtypeStruct((8, 64, outchans), BF),
        in_specs=[VMEM] * 4,
        out_specs=VMEM,
        scratch_shapes=[pltpu.VMEM((40, outchans), F32), pltpu.VMEM((chans // 128, 64, 128), F32)],
        compiler_params=pltpu.CompilerParams(vmem_limit_bytes=12 * 1024 * 1024),
        cost_estimate=pl.CostEstimate(flops=120000000, bytes_accessed=3500000, transcendentals=0),
    )(sums, proj_a, proj_b, conv_w)


def pair_block(flags, pair, cot, top, bottom, halos, rowp, bins, ahead, back):
    chans = 128
    return pl.pallas_call(
        pair_kernel,
        out_shape=(
            jax.ShapeDtypeStruct((32, 64, chans), BF),
            jax.ShapeDtypeStruct((KEPT, chans), F32),
            jax.ShapeDtypeStruct((KEPT, chans), BF),
            jax.ShapeDtypeStruct((40, chans), BF),
        ),
        in_specs=[SMEM] + [VMEM] * 9,
        out_specs=(VMEM,) * 4,
        scratch_shapes=[
            pltpu.VMEM((38, 96, chans), F32),
            pltpu.VMEM((38, WIDE, 3 * chans), BF),
            pltpu.VMEM((36, WIDE, chans), F32),
            pltpu.VMEM((36, 96, chans), F32),
            pltpu.VMEM((36, WIDE, 3 * chans), BF),
            pltpu.VMEM((9 * chans, chans), F32),
            pltpu.VMEM((72, chans), F32),
            pltpu.VMEM((96, chans), F32),
            pltpu.VMEM((384, chans), F32),
            pltpu.VMEM((38, 8, chans), F32),
            pltpu.VMEM((38, 8, chans), F32),
        ],
        compiler_params=pltpu.CompilerParams(vmem_limit_bytes=24 * 1024 * 1024),
        cost_estimate=pl.CostEstimate(flops=2500000000, bytes_accessed=4000000, transcendentals=700000),
    )(flags, pair, cot, top, bottom, halos, rowp, bins, ahead, back)


def local(fine, conv_w, proj_a, proj_b, pair_in, pair_w, cotangent):
    pairs = pair_in.shape[3]
    row, col = lax.axis_index("row"), lax.axis_index("col")
    core, zpos = row % 2, row // 2
    place = jnp.arange(8)
    place, spot, most = place // 2, jnp.where(place < 2, row, jnp.where(place < 4, col, core)), place % 2
    flags = jnp.where(most == 0, spot > 0, spot < jnp.where(place == 0, 15, 7)).astype(jnp.int32)

    fine, pair, cot = fine[0], pair_in[0], cotangent[0]
    apart = (zpos - col) & 7
    is_there = [jnp.where(core == 0, apart == far, (apart == 8 - far) & (far < 4)) for far in (1, 2, 3, 4)]
    is_held = (apart == 0) | ((apart <= 4) == (core == 0))
    scalars = (core == 0, is_there, is_held, zpos == col, [(zpos ^ k) & 3 for k in range(4)], col % 2 == 1)
    scalars += ([(col // 2 + k) & 3 for k in range(4)],)
    seed, flags, scalars = lax.optimization_barrier((jnp.zeros((8, 128), F32), flags, scalars))
    is_first, is_there, is_held, is_root, places, is_odd, ahead = scalars
    down, above = ends(fine, pair, cot, begin(seed))
    top, bottom = shift(down, "row", 1), shift(above, "row", -1)
    weight = pair_w.reshape(9 * pairs, pairs)
    top, bottom, weights = lax.optimization_barrier((top, bottom, two_row_weights(weight)))
    to_next, to_last = conv_forward(flags, fine, top, bottom, conv_w, proj_a, proj_b, pair, cot)

    across, from_last, from_next = shift(to_next[:80], "col", 4), shift(to_next, "col", 2), shift(to_last, "col", -2)
    both = ((up(to_next[:80]) + up(across)) + (up(from_last[:80]) + up(from_next[:80]))).astype(BF)
    to_left = jnp.where(is_odd, from_last[80:], to_next[80:])
    to_right = jnp.where(is_odd, to_last[80:], from_next[80:])
    other = flip(jnp.concatenate([both, to_left, to_right]), "col", 1)
    both, halos = up(both) + up(other[:80]), other[80:]
    rowp, colp_here = both[:40], both[40:].astype(BF)

    mine = jnp.where(is_first, colp_here[:35], colp_here[3:38])
    other = flip(mine, "row", 1)
    colp = jnp.concatenate([jnp.where(is_first, mine, other), jnp.where(is_first, other, mine)])
    sent = [spread(colp, far) for far in (4, 3, 2, 1)]
    for far, got in zip((4, 3, 2, 1), sent):
        colp = jnp.where(is_there[far - 1], got, colp)
    colp = jnp.where(is_held, colp, flip(colp, "row", 1))
    out, keep, send, rowg = pair_block(flags, pair, cot, top, bottom, halos, rowp, up(colp), *weights)

    total = (keep + up(flip(send, "row", 1))).astype(BF)
    half, colg = total[:576].reshape(4, 144, pairs), total[576:]

    def quarter(k):
        return taken(half, places[k])

    def joined(k):
        return jnp.concatenate([quarter(k), colg])

    got = [flip(joined(k), "row", 2 * k) for k in (1, 2, 3)]
    total = ((up(joined(0)) + up(got[0])) + (up(got[1]) + up(got[2]))).astype(BF)
    total = sum_flip(total, "row", 8)
    colg = jnp.where(is_root, total[144:], 0)
    total = sum_y(jnp.concatenate([total[:144], rowg, colg]))

    quart = total[:144]
    across, others = flip(total, "col", 1), flip(quart, "batch", 1)
    crossed = lax.ppermute(quart, ("col", "batch"), [(i, i ^ 3) for i in range(16)])
    sums = (up(total[144:]) + up(across[144:])).astype(BF)
    parts = conv_backward(sums, proj_a, proj_b, conv_w)
    parts, quart = lax.optimization_barrier((parts, quart))
    quart = ((up(quart) + up(across[:144])) + (up(others) + up(crossed))).astype(BF)

    parts = parts.reshape(4, 128, parts.shape[2])
    got = [shift(taken(parts, ahead[k]), "col", 2 * k) for k in (1, 2, 3)]
    near = {k: flip(quart, "row", 2 * k) for k in (1,)}
    got, quart, near = lax.optimization_barrier((got, quart, near))
    mine = (up(taken(parts, ahead[0])) + up(got[0])) + (up(got[1]) + up(got[2]))
    near.update({k: flip(quart, "row", 2 * k) for k in (2, 3)})
    near = jnp.stack([quart, near[1], near[2], near[3]])
    other = flip(jnp.where(is_odd, mine[:64], mine[64:]).astype(BF), "col", 1)
    half = jnp.concatenate([taken(near, places[k]) for k in range(4)])
    theirs = flip(half, "row", 1)
    grad_pair_w = jnp.concatenate([jnp.where(is_first, half, theirs), jnp.where(is_first, theirs, half)])
    grad_pair_w = up(grad_pair_w).reshape(3, 3, pairs, pairs) / 512.0
    grad_fine = (jnp.where(is_odd, mine[64:], mine[:64]) + up(other)).astype(BF)
    return out[None], grad_fine[None], grad_pair_w


def solution(mesh):
    return jax.shard_map(
        local,
        mesh=mesh,
        in_specs=(
            P("batch", "row", None),
            P(None, "col", None),
            P("col", None),
            P("col", None),
            P("batch", "row", "col", None),
            P(),
            P("batch", "row", "col", None),
        ),
        out_specs=(P("batch", "row", "col", None), P("batch", "row", "col"), P()),
        check_vma=False,
    )
```

```python
import jax
import jax.numpy as jnp
from jax import lax
from jax.experimental import pallas as pl
from jax.experimental.pallas import tpu as pltpu
from jax.sharding import PartitionSpec as P

BF = jnp.bfloat16
F32 = jnp.float32
WIDE = 80
STEP = 3
KEPT = 616


def shift(x, axis, step):
    count = lax.axis_size(axis)
    return lax.ppermute(x, axis, [(i, (i + step) % count) for i in range(count)])


def flip(x, axis, bit):
    count = lax.axis_size(axis)
    return lax.ppermute(x, axis, [(i, i ^ bit) for i in range(count)])


def spread(x, far):
    def place(z, core, col):
        return (z % 8 * 2 + core) * 8 + col

    pairs = {}
    for col in range(8):
        pairs[place(col, 0, col)] = place(col + far, 0, col)
        if far < 4:
            pairs[place(col, 1, col)] = place(col - far, 1, col)
    open_ends = set(range(128)) - set(pairs.values())
    for at in range(128):
        if at not in pairs and at ^ 8 in open_ends:
            pairs[at] = at ^ 8
            open_ends.remove(at ^ 8)
    for at in range(128):
        if at not in pairs:
            pairs[at] = min(end for end in open_ends if end % 8 == at % 8)
            open_ends.remove(pairs[at])
    return lax.ppermute(x, ("row", "col"), sorted(pairs.items()))


def up(x):
    return x.astype(F32)


def sum_y(x):
    across, left, right = shift(x, "col", 4), shift(x, "col", 2), shift(x, "col", 6)
    return ((up(x) + up(across)) + (up(left) + up(right))).astype(BF)


def sum_flip(x, axis, bit):
    return (up(x) + up(flip(x, axis, bit))).astype(BF)


def taken(x, at):
    return lax.dynamic_slice(x, (at, 0, 0), (1,) + x.shape[1:], allow_negative_indices=False)[0]


def pair_kernel(
    flags, pair, cot, top, bottom, halos, rowp, bins, ahead, back,
    out, keep, send, rowg,
    zwide, z3, cots, qwide, q3, wgrad, line, colp, packed, left, right,
):
    chans = 128
    has_up, has_down, has_left, has_right, core = (flags[i] for i in range(5))
    rows = lax.broadcasted_iota(jnp.int32, (38, 1, 1), 0)
    row_ok = ((rows >= 3) | (has_up > 0)) & ((rows < 35) | (has_down > 0))

    colp[...] = jnp.zeros((96, chans), F32)
    colp[5:75] = bins[0:70]
    colp[85:88] = bins[0:3]
    colp[88:89] = bins[3:4]

    packed[...] = up(halos[...])
    for i in range(38):
        left[i, 0:5] = packed[5 * i : 5 * i + 5]
        right[i, 0:5] = packed[192 + 5 * i : 197 + 5 * i]

    zwide[:, 0:8] = jnp.zeros((38, 8, chans), F32)
    zwide[:, 72:96] = jnp.zeros((38, 24, chans), F32)
    cots[:, 64:80] = jnp.zeros((36, 16, chans), F32)

    def zeta(values, first, count, lo, hi):
        scaled = rowp[first : first + count][:, None, :] * colp[lo:hi][None, :, :]
        return up((up(values) + scaled).astype(BF))

    zwide[0:3, 8:72] = jnp.where(has_up > 0, zeta(top[3:6], 0, 3, 8, 72), 0.0)
    zwide[35:38, 8:72] = jnp.where(has_down > 0, zeta(bottom[3:6], 35, 3, 8, 72), 0.0)
    cots[0:2, 0:64] = jnp.where(has_up > 0, up(top[6:8]), 0.0)
    cots[34:36, 0:64] = jnp.where(has_down > 0, up(bottom[6:8]), 0.0)
    edge = jnp.where(row_ok & (has_left > 0), zeta(left[:, 0:3], 0, 38, 5, 8), 0.0)
    zwide[:, 5:8] = edge
    zwide[:, 85:88] = edge
    edge = jnp.where(row_ok & (has_right > 0), zeta(right[:, 0:3], 0, 38, 72, 75), 0.0)
    zwide[:, 72:75] = edge
    cots[:, 78:80] = jnp.where(row_ok[1:37] & (has_left > 0), up(left[1:37, 3:5]), 0.0)
    cots[:, 64:66] = jnp.where(row_ok[1:37] & (has_right > 0), up(right[1:37, 3:5]), 0.0)
    for at in range(0, 32, 4):
        zwide[at + 3 : at + 7, 8:72] = zeta(pair[at : at + 4], at + 3, 4, 8, 72)
        cots[at + 2 : at + 6, 0:64] = up(cot[at : at + 4])
    zwide[:, 88:89] = zwide[:, 8:9]
    for at in range(0, 38, 2):
        for across in range(3):
            z3[at : at + 2, :, across * chans : (across + 1) * chans] = zwide[
                at : at + 2, 7 + across : 87 + across
            ].astype(BF)

    qwide[:, 0:8] = jnp.zeros((36, 8, chans), F32)
    qwide[:, 88:96] = jnp.zeros((36, 8, chans), F32)

    def taps(ref, at, count):
        rows = [jnp.concatenate([ref[at + 2 * i + d] for i in range(count)]) for d in range(4)]
        return jnp.concatenate(rows, axis=1)

    for at in range(0, 36, 2 * STEP):
        both = jnp.dot(taps(z3, at, STEP), ahead[...], preferred_element_type=F32)
        for half in range(2):
            for i in range(STEP):
                row = at + 2 * i + half
                hidden = both[i * WIDE : (i + 1) * WIDE, half * chans : (half + 1) * chans]
                sigma = jax.nn.sigmoid(hidden)
                grown = hidden * sigma
                q = cots[row] * (sigma + grown * (1.0 - sigma))
                qwide[row, 8:88] = up(q.astype(BF))
                if 2 <= row < 34:
                    out[row - 2] = (zwide[row + 1, 8:72] + grown[0:64]).astype(BF)
    qwide[:, 7:8] = qwide[:, 87:88]
    qwide[:, 88:89] = qwide[:, 8:9]
    for at in range(0, 36, 2):
        for across in range(3):
            q3[at : at + 2, :, across * chans : (across + 1) * chans] = qwide[
                at : at + 2, 9 - across : 89 - across
            ].astype(BF)

    own = q3[2:34, 0:64, chans : 2 * chans].reshape(2048, chans)
    for down in range(3):
        near = z3[down + 2 : down + 34, 0:64].reshape(2048, 3 * chans)
        part = lax.dot_general(own, near, (((0,), (0,)), ((), ())), preferred_element_type=F32)
        for across in range(3):
            at = (3 * down + across) * chans
            wgrad[at : at + chans] = part[:, across * chans : (across + 1) * chans].T

    total = jnp.zeros((WIDE, chans), F32)
    sums = {}
    for at in range(0, 34, 2 * STEP):
        count = min(STEP, (34 - at) // 2)
        both = jnp.dot(taps(q3, at, count), back[...], preferred_element_type=F32)
        for half in range(2):
            for i in range(count):
                row = at + 2 * i + half
                zgrad = both[i * WIDE : (i + 1) * WIDE, half * chans : (half + 1) * chans] + cots[row + 1]
                sums[row] = jnp.sum(zgrad[0:64] * colp[8:72], axis=0, keepdims=True)
                if 1 <= row < 33:
                    total = total + zgrad * rowp[row + 2 : row + 3]
    sums[0] = jnp.where(has_up > 0, sums[0], 0.0)
    sums[33] = jnp.where(has_down > 0, sums[33], 0.0)
    rowg[...] = jnp.concatenate([sums[row] for row in range(34)] + [jnp.zeros((6, chans), F32)]).astype(BF)
    line[0:1] = jnp.where(has_left > 0, total[79:80], 0.0)
    line[1:65] = total[0:64]
    line[65:66] = jnp.where(has_right > 0, total[64:65], 0.0)
    keep[576:616] = jnp.zeros((40, chans), F32)
    send[576:616] = jnp.zeros((40, chans), BF)
    for mine in range(2):

        @pl.when(core == mine)
        def _(mine=mine):
            keep[0:576] = wgrad[576 * mine : 576 * mine + 576]
            send[0:576] = wgrad[576 - 576 * mine : 1152 - 576 * mine].astype(BF)
            keep[576:610] = line[32 * mine : 32 * mine + 34]
            send[576:610] = line[32 - 32 * mine : 66 - 32 * mine].astype(BF)


def run_all(copies):
    for copy in copies:
        copy.start()
    for copy in copies:
        copy.wait()


def turn_kernel(weight, ahead, back):
    chans = 128
    size = 3 * chans
    for row in range(4):
        here = slice(size * row, size * row + size)
        for out in range(2):
            lanes = slice(chans * out, chans * out + chans)
            tap = row - out
            if 0 <= tap < 3:
                ahead[here, lanes] = weight[size * tap : size * tap + size]
                for across in range(3):
                    at = size * (2 - tap) + chans * across
                    turned = up(weight[at : at + chans]).T.astype(BF)
                    back[size * row + chans * across : size * row + chans * across + chans, lanes] = turned
            else:
                ahead[here, lanes] = jnp.zeros((size, chans), BF)
                back[here, lanes] = jnp.zeros((size, chans), BF)


def begin_kernel(given, taken):
    taken[...] = given[...]


def ends_kernel(fine, pair, cot, begun, to_next, to_last, sems):
    copies = []

    def add(source, target):
        copies.append(pltpu.make_async_copy(source, target, sems.at[len(copies)]))

    blocks = fine.shape[1] // 128
    for ref, spots, pair_rows, cot_rows in ((to_next, 48, 29, 30), (to_last, 0, 0, 0)):
        for j in range(blocks):
            add(fine.at[spots : spots + 16, 128 * j : 128 * j + 128], ref.at[j // 4, 16 * (j % 4) : 16 * (j % 4) + 16])
        add(pair.at[pair_rows : pair_rows + 3], ref.at[3:6])
        add(cot.at[cot_rows : cot_rows + 2], ref.at[6:8])
    run_all(copies)


def conv_kernel(
    flags, fine, top, bottom, conv_w, proj_a, proj_b, pair, cot,
    to_next, to_last, wide, edge,
):
    blocks = wide.shape[0]
    wide[:, 80:88] = jnp.zeros((blocks, 8, 128), F32)
    for j in range(blocks):
        lanes = slice(128 * j, 128 * j + 128)
        spots = up(top[j // 4, 16 * (j % 4) : 16 * (j % 4) + 16])
        wide[j, 0:8] = jnp.where(flags[0] > 0, spots[8:], 0.0)
        wide[j, 8:72] = up(fine[:, lanes])
        spots = up(bottom[j // 4, 16 * (j % 4) : 16 * (j % 4) + 16])
        wide[j, 72:80] = jnp.where(flags[1] > 0, spots[:8], 0.0)
    seq = jnp.zeros((40, conv_w.shape[1]), F32)
    for tap in range(5):
        window = jnp.concatenate([wide[j, pl.ds(tap, 40, stride=2)] for j in range(blocks)], axis=1)
        seq = seq + lax.dot_general(
            window.astype(BF), conv_w[tap], (((1,), (1,)), ((), ())), preferred_element_type=F32
        )
    rows = lax.broadcasted_iota(jnp.int32, (40, 1), 0)
    ok = ((rows >= 3) | (flags[0] > 0)) & ((rows < 35) | (flags[1] > 0)) & (rows < 38)
    seq = jnp.where(ok, seq, 0.0).astype(BF)
    rowp = jnp.dot(seq, proj_a[...], preferred_element_type=F32).astype(BF)
    colp = jnp.dot(seq, proj_b[...], preferred_element_type=F32).astype(BF)
    for ref in (to_next, to_last):
        ref[0:40] = rowp
        ref[40:80] = colp

    edge[...] = jnp.zeros(edge.shape, F32)
    for ref, pair_cols, cot_cols in ((to_next, (61, 64), (62, 64)), (to_last, (0, 3), (0, 2))):
        for i in range(38):
            if i < 3:
                ours, theirs = top[i + 3 : i + 4], top[i + 5 : i + 6]
            elif i < 35:
                ours, theirs = pair[i - 3 : i - 2], cot[i - 3 : i - 2]
            else:
                ours, theirs = bottom[i - 32 : i - 31], bottom[min(i - 29, 7) : min(i - 28, 8)]
            edge[5 * i : 5 * i + 3] = up(ours[0, pair_cols[0] : pair_cols[1]])
            edge[5 * i + 3 : 5 * i + 5] = up(theirs[0, cot_cols[0] : cot_cols[1]])
        ref[80:272] = edge[...].astype(BF)


def grad_conv_kernel(sums, proj_a, proj_b, conv_w, parts, seqg, whole):
    grad = sum(
        lax.dot_general(x, proj[...], (((1,), (1,)), ((), ())), preferred_element_type=F32)
        for x, proj in ((sums[0:40], proj_a), (sums[40:80], proj_b))
    )
    seqg[...] = up(grad.astype(BF))
    ahead, here, behind = (seqg[at : at + 32].astype(BF) for at in (2, 1, 0))

    def times(x, tap):
        return jnp.dot(x, conv_w[tap], preferred_element_type=F32)

    even = times(ahead, 0) + times(here, 2) + times(behind, 4)
    odd = times(ahead, 1) + times(here, 3)
    for j in range(whole.shape[0]):
        lanes = slice(128 * j, 128 * j + 128)
        whole[j, pl.ds(0, 32, stride=2)] = even[:, lanes]
        whole[j, pl.ds(1, 32, stride=2)] = odd[:, lanes]
    for m in range(4):
        low, middle, high = (whole[3 * m + i] for i in range(3))
        parts[2 * m] = jnp.concatenate([low, middle[:, :64]], axis=1).astype(BF)
        parts[2 * m + 1] = jnp.concatenate([middle[:, 64:], high], axis=1).astype(BF)


VMEM = pl.BlockSpec(memory_space=pltpu.VMEM)
SMEM = pl.BlockSpec(memory_space=pltpu.SMEM)


HBM = pl.BlockSpec(memory_space=pltpu.HBM)


def two_row_weights(weight):
    shape = jax.ShapeDtypeStruct((12 * weight.shape[1], 2 * weight.shape[1]), BF)
    return pl.pallas_call(
        turn_kernel,
        out_shape=(shape, shape),
        in_specs=[VMEM],
        out_specs=(VMEM, VMEM),
        compiler_params=pltpu.CompilerParams(vmem_limit_bytes=6 * 1024 * 1024),
        cost_estimate=pl.CostEstimate(flops=40000000000, bytes_accessed=600000, transcendentals=0),
    )(weight)


def begin(seed):
    return pl.pallas_call(
        begin_kernel,
        out_shape=jax.ShapeDtypeStruct(seed.shape, seed.dtype),
        in_specs=[VMEM],
        out_specs=VMEM,
        compiler_params=pltpu.CompilerParams(vmem_limit_bytes=1024 * 1024),
        cost_estimate=pl.CostEstimate(flops=40000000000, bytes_accessed=8192, transcendentals=0),
    )(seed)


def ends(fine, pair, cot, begun):
    payload = jax.ShapeDtypeStruct((8, 64, 128), BF)
    return pl.pallas_call(
        ends_kernel,
        out_shape=(payload, payload),
        in_specs=[VMEM] * 4,
        out_specs=(VMEM, VMEM),
        scratch_shapes=[pltpu.SemaphoreType.DMA((2 * (fine.shape[1] // 128) + 4,))],
        compiler_params=pltpu.CompilerParams(vmem_limit_bytes=6 * 1024 * 1024),
        cost_estimate=pl.CostEstimate(flops=0, bytes_accessed=600000, transcendentals=0),
    )(fine, pair, cot, begun)


def conv_forward(*arrays):
    chans = arrays[1].shape[1]
    payload = jax.ShapeDtypeStruct((272, 128), BF)
    return pl.pallas_call(
        conv_kernel,
        out_shape=(payload, payload),
        in_specs=[SMEM] + [VMEM] * 8,
        out_specs=(VMEM, VMEM),
        scratch_shapes=[pltpu.VMEM((chans // 128, 88, 128), F32), pltpu.VMEM((192, 128), F32)],
        compiler_params=pltpu.CompilerParams(vmem_limit_bytes=12 * 1024 * 1024),
        cost_estimate=pl.CostEstimate(flops=120000000, bytes_accessed=3500000, transcendentals=0),
    )(*arrays)


def conv_backward(sums, proj_a, proj_b, conv_w):
    outchans, chans = conv_w.shape[1:]
    return pl.pallas_call(
        grad_conv_kernel,
        out_shape=jax.ShapeDtypeStruct((8, 64, outchans), BF),
        in_specs=[VMEM] * 4,
        out_specs=VMEM,
        scratch_shapes=[pltpu.VMEM((40, outchans), F32), pltpu.VMEM((chans // 128, 64, 128), F32)],
        compiler_params=pltpu.CompilerParams(vmem_limit_bytes=12 * 1024 * 1024),
        cost_estimate=pl.CostEstimate(flops=120000000, bytes_accessed=3500000, transcendentals=0),
    )(sums, proj_a, proj_b, conv_w)


def pair_block(flags, pair, cot, top, bottom, halos, rowp, bins, ahead, back):
    chans = 128
    return pl.pallas_call(
        pair_kernel,
        out_shape=(
            jax.ShapeDtypeStruct((32, 64, chans), BF),
            jax.ShapeDtypeStruct((KEPT, chans), F32),
            jax.ShapeDtypeStruct((KEPT, chans), BF),
            jax.ShapeDtypeStruct((40, chans), BF),
        ),
        in_specs=[SMEM] + [VMEM] * 9,
        out_specs=(VMEM,) * 4,
        scratch_shapes=[
            pltpu.VMEM((38, 96, chans), F32),
            pltpu.VMEM((38, WIDE, 3 * chans), BF),
            pltpu.VMEM((36, WIDE, chans), F32),
            pltpu.VMEM((36, 96, chans), F32),
            pltpu.VMEM((36, WIDE, 3 * chans), BF),
            pltpu.VMEM((9 * chans, chans), F32),
            pltpu.VMEM((72, chans), F32),
            pltpu.VMEM((96, chans), F32),
            pltpu.VMEM((384, chans), F32),
            pltpu.VMEM((38, 8, chans), F32),
            pltpu.VMEM((38, 8, chans), F32),
        ],
        compiler_params=pltpu.CompilerParams(vmem_limit_bytes=24 * 1024 * 1024),
        cost_estimate=pl.CostEstimate(flops=2500000000, bytes_accessed=4000000, transcendentals=700000),
    )(flags, pair, cot, top, bottom, halos, rowp, bins, ahead, back)


def local(fine, conv_w, proj_a, proj_b, pair_in, pair_w, cotangent):
    pairs = pair_in.shape[3]
    row, col = lax.axis_index("row"), lax.axis_index("col")
    core, zpos = row % 2, row // 2
    place = jnp.arange(8)
    place, spot, most = place // 2, jnp.where(place < 2, row, jnp.where(place < 4, col, core)), place % 2
    flags = jnp.where(most == 0, spot > 0, spot < jnp.where(place == 0, 15, 7)).astype(jnp.int32)

    fine, pair, cot = fine[0], pair_in[0], cotangent[0]
    apart = (zpos - col) & 7
    is_there = [jnp.where(core == 0, apart == far, (apart == 8 - far) & (far < 4)) for far in (1, 2, 3, 4)]
    is_held = (apart == 0) | ((apart <= 4) == (core == 0))
    scalars = (core == 0, is_there, is_held, zpos == col, [(zpos ^ k) & 3 for k in range(4)], col % 2 == 1)
    scalars += ([(col // 2 + k) & 3 for k in range(4)],)
    seed, flags, scalars = lax.optimization_barrier((jnp.zeros((8, 128), F32), flags, scalars))
    is_first, is_there, is_held, is_root, places, is_odd, ahead = scalars
    down, above = ends(fine, pair, cot, begin(seed))
    top, bottom = shift(down, "row", 1), shift(above, "row", -1)
    weight = pair_w.reshape(9 * pairs, pairs)
    top, bottom, weights = lax.optimization_barrier((top, bottom, two_row_weights(weight)))
    to_next, to_last = conv_forward(flags, fine, top, bottom, conv_w, proj_a, proj_b, pair, cot)

    across, from_last, from_next = shift(to_next[:80], "col", 4), shift(to_next, "col", 2), shift(to_last, "col", -2)
    both = ((up(to_next[:80]) + up(across)) + (up(from_last[:80]) + up(from_next[:80]))).astype(BF)
    to_left = jnp.where(is_odd, from_last[80:], to_next[80:])
    to_right = jnp.where(is_odd, to_last[80:], from_next[80:])
    other = flip(jnp.concatenate([both, to_left, to_right]), "col", 1)
    both, halos = up(both) + up(other[:80]), other[80:]
    rowp, colp_here = both[:40], both[40:].astype(BF)

    mine = jnp.where(is_first, colp_here[:35], colp_here[3:38])
    other = flip(mine, "row", 1)
    colp = jnp.concatenate([jnp.where(is_first, mine, other), jnp.where(is_first, other, mine)])
    sent = [spread(colp, far) for far in (4, 3, 2, 1)]
    for far, got in zip((4, 3, 2, 1), sent):
        colp = jnp.where(is_there[far - 1], got, colp)
    colp = jnp.where(is_held, colp, flip(colp, "row", 1))
    out, keep, send, rowg = pair_block(flags, pair, cot, top, bottom, halos, rowp, up(colp), *weights)

    total = (keep + up(flip(send, "row", 1))).astype(BF)
    half, colg = total[:576].reshape(4, 144, pairs), total[576:]

    def quarter(k):
        return taken(half, places[k])

    def joined(k):
        return jnp.concatenate([quarter(k), colg])

    got = [flip(joined(k), "row", 2 * k) for k in (1, 2, 3)]
    total = ((up(joined(0)) + up(got[0])) + (up(got[1]) + up(got[2]))).astype(BF)
    total = sum_flip(total, "row", 8)
    colg = jnp.where(is_root, total[144:], 0)
    total = sum_y(jnp.concatenate([total[:144], rowg, colg]))

    quart = total[:144]
    across, others = flip(total, "col", 1), flip(quart, "batch", 1)
    crossed = lax.ppermute(quart, ("col", "batch"), [(i, i ^ 3) for i in range(16)])
    sums = (up(total[144:]) + up(across[144:])).astype(BF)
    parts = conv_backward(sums, proj_a, proj_b, conv_w)
    parts, quart = lax.optimization_barrier((parts, quart))
    quart = ((up(quart) + up(across[:144])) + (up(others) + up(crossed))).astype(BF)

    parts = parts.reshape(4, 128, parts.shape[2])
    got = [shift(taken(parts, ahead[k]), "col", 2 * k) for k in (1, 2, 3)]
    near = {k: flip(quart, "row", 2 * k) for k in (1,)}
    got, quart, near = lax.optimization_barrier((got, quart, near))
    mine = (up(taken(parts, ahead[0])) + up(got[0])) + (up(got[1]) + up(got[2]))
    near.update({k: flip(quart, "row", 2 * k) for k in (2, 3)})
    near = jnp.stack([quart, near[1], near[2], near[3]])
    other = flip(jnp.where(is_odd, mine[:64], mine[64:]).astype(BF), "col", 1)
    half = jnp.concatenate([taken(near, places[k]) for k in range(4)])
    theirs = flip(half, "row", 1)
    grad_pair_w = jnp.concatenate([jnp.where(is_first, half, theirs), jnp.where(is_first, theirs, half)])
    grad_pair_w = up(grad_pair_w).reshape(3, 3, pairs, pairs) / 512.0
    other, grad_pair_w = lax.optimization_barrier((other, grad_pair_w))
    grad_fine = (jnp.where(is_odd, mine[64:], mine[:64]) + up(other)).astype(BF)
    return out[None], grad_fine[None], grad_pair_w


def solution(mesh):
    return jax.shard_map(
        local,
        mesh=mesh,
        in_specs=(
            P("batch", "row", None),
            P(None, "col", None),
            P("col", None),
            P("col", None),
            P("batch", "row", "col", None),
            P(),
            P("batch", "row", "col", None),
        ),
        out_specs=(P("batch", "row", "col", None), P("batch", "row", "col"), P()),
        check_vma=False,
    )
```
